32 devices in a mesh: dp: 8 (over z, x), ctx: 4 (over y, core).
Axes of the slice: x: 2, y: 2, z: 4, core: 2. Of those that a mesh axis runs over, the one named last changes fastest.
Arguments:
- layer_input: bfloat16 [8, 512, 4096], P('dp', 'ctx'), may hold values from -6 to 6
- queries: bfloat16 [8, 512, 4096], P('dp', 'ctx'), may hold values from -4.5 to 4.5
- keys_saved: bfloat16 [8, 512, 1024], P('dp', 'ctx'), may hold values from -4.5 to 4.5
- values_saved: bfloat16 [8, 512, 1024], P('dp', 'ctx'), may hold values from -6 to 6
- out_grad: bfloat16 [8, 512, 4096], P('dp', 'ctx'), may hold values from -6 to 6
- master_weight: float32 [4096, 6144], P('dp', 'ctx'), may hold values from -2 to 2
- first_moment: float32 [4096, 6144], P('dp', 'ctx'), may hold values from -100 to 100
- second_moment: float32 [4096, 6144], P('dp', 'ctx'), may hold values from 10 to 3000
Outputs:
- first_new: float32 [4096, 6144], P('dp', 'ctx')
- second_new: float32 [4096, 6144], P('dp', 'ctx')
- lamb_update: float32 [4096, 6144], P('dp', 'ctx')
- new_weights: bfloat16 [4096, 6144], P(None, 'ctx')
The draws below stay inside these ranges and needn't reach their ends.
All inputs are finite; a program needn't handle non-finite values.
Results may differ from the reference program's by a relative error of at most 0.0095.
Values may be sent and summed in bfloat16 or wider, within the bound.
A program may use at most 128 MiB of HBM per device.

```python
import math
import jax
import jax.numpy as jnp
from jax import lax

D = 4096
HEADS = 32
KV_HEADS = 8
HEAD_DIM = 128
STEP = 100
BATCH = 8
SEQ_LEN = 512
GROUP = 4
QKV_COLS = 6144


def draw_queries(key, part):
    shape = (BATCH, SEQ_LEN, HEADS * HEAD_DIM)
    values = jnp.clip(jax.random.normal(jax.random.fold_in(key, 12), shape, jnp.float32), -4.0, 4.0)
    return values.astype(jnp.bfloat16)


def draw_keys_saved(key, part):
    shape = (BATCH, SEQ_LEN, KV_HEADS * HEAD_DIM)
    values = jnp.clip(jax.random.normal(jax.random.fold_in(key, 22), shape, jnp.float32), -4.0, 4.0)
    return values.astype(jnp.bfloat16)


def scaled_matrix(key, divisor, limit):
    row_scale = 10.0 ** (jnp.arange(D, dtype=jnp.float32) / D)
    base = jnp.clip(jax.random.normal(jax.random.fold_in(key, 32), (D, QKV_COLS), jnp.float32), -4.0, 4.0)
    col_scale = 10.0 ** jax.random.uniform(jax.random.fold_in(key, 33), (QKV_COLS,), jnp.float32)
    return jnp.clip(base * row_scale[:, None] * col_scale[None, :] / divisor, -limit, limit)


def draw_master_weight(key, part):
    return scaled_matrix(jax.random.fold_in(key, 41), 3.0 * D ** 0.5, 2.0)


def draw_first_moment(key, part):
    return scaled_matrix(jax.random.fold_in(key, 42), 1.0, 100.0)


def spiked(values, stream_key, source, target, shards_of, factor):
    owner, partner = [(jnp.arange(values.shape[position]) // (values.shape[position] // shards_of)).reshape([-1 if axis == position else 1 for axis in range(values.ndim)]) for position in (source, target)]
    chosen = jax.random.permutation(stream_key, shards_of)[partner]
    strong = (owner == chosen) | (owner == (partner + shards_of // 2) % shards_of)
    return jnp.where(strong, factor * values, values)


def levels(own_key, dims, shards, low, top_value):
    level = 1.0
    for dim, shards_of in shards:
        heights = jax.random.uniform(jax.random.fold_in(jax.random.fold_in(own_key, 6), dim), (shards_of,), jnp.float32, low / len(shards), top_value / len(shards))
        level = level * jnp.repeat(jnp.exp(heights), dims[dim] // shards_of).reshape((-1,) + (1,) * (len(dims) - 1 - dim))
    return level


def scatter_about(own_key, extent, width, most, pieces=(), kind=jnp.bfloat16):
    drawn = jax.random.normal(own_key, extent, jnp.float32) * width
    if len(pieces) > 0:
        drawn = levels(own_key, extent, pieces, -0.22, 0.18) * drawn
    return jnp.clip(drawn, min=-most, max=most).astype(kind)


def heavy_noise(rng, dims, deviation, most, split, heavy, kind=jnp.bfloat16):
    drawn = deviation * jax.random.normal(rng, dims, jnp.float32)
    if split:
        drawn = drawn * levels(rng, dims, split, -0.22, 0.18)
    return jnp.clip(spiked(drawn, jax.random.fold_in(rng, 3), *heavy), -most, most).astype(kind)


def setup_inputs(seed: int = 0) -> dict:
    streams_of = jax.random.split(jax.random.key(seed), 9)
    return {
        "layer_input": heavy_noise(streams_of[0], (BATCH, SEQ_LEN, D), 1.0, 6.0, ((0, 8), (1, 4)), (0, 2, 8, 2.0)),
        "queries": draw_queries(jax.random.fold_in(streams_of[8], 71), 0),
        "keys_saved": draw_keys_saved(jax.random.fold_in(streams_of[8], 71), 0),
        "values_saved": scatter_about(streams_of[3], (BATCH, SEQ_LEN, KV_HEADS * HEAD_DIM), 1.0, 6.0, ((0, 8), (1, 4))),
        "out_grad": scatter_about(streams_of[4], (BATCH, SEQ_LEN, HEADS * HEAD_DIM), 1.0, 6.0, ((0, 8), (1, 4))),
        "master_weight": draw_master_weight(jax.random.fold_in(streams_of[8], 71), 0),
        "first_moment": draw_first_moment(jax.random.fold_in(streams_of[8], 71), 0),
        "second_moment": jnp.clip(jnp.exp(math.log(3000.0) - 5.7037825 * jax.random.uniform(streams_of[7], (D, QKV_COLS), jnp.float32) ** levels(streams_of[7], (D, QKV_COLS), ((0, 8), (1, 4)), -0.2, 0.2)), 10.0, 3000.0),
    }


beta_first = 0.9
beta_second = 0.999
adam_epsilon = 1e-06
decay_rate = 0.01
learn_rate = 0.01
masked_score = -1e+30

def sequence_grads(query_seq, key_seq, value_seq, grad_seq):
    length = query_seq.shape[0]
    score_scale = HEAD_DIM ** (-0.5)
    query_f = query_seq.astype(jnp.float32).reshape(length, KV_HEADS, GROUP, HEAD_DIM)
    key_f = key_seq.astype(jnp.float32).reshape(length, KV_HEADS, HEAD_DIM)
    value_f = value_seq.astype(jnp.float32).reshape(length, KV_HEADS, HEAD_DIM)
    grad_f = grad_seq.astype(jnp.float32).reshape(length, KV_HEADS, GROUP, HEAD_DIM)
    scores = jnp.einsum('qgrd,kgd->grqk', query_f, key_f) * score_scale
    positions = jnp.arange(length)
    allowed = positions[None, :] <= positions[:, None]
    scores = jnp.where(allowed, scores, masked_score)
    probabilities = jax.nn.softmax(scores, axis=-1)
    probs_b = probabilities.astype(jnp.bfloat16).astype(jnp.float32)
    attended = jnp.einsum('grqk,kgd->qgrd', probs_b, value_f)
    row_delta = lax.optimization_barrier(jnp.sum(grad_f * attended, axis=-1))
    prob_grad = jnp.einsum('qgrd,kgd->grqk', grad_f, value_f)
    dscore = probabilities * (prob_grad - jnp.transpose(row_delta, (1, 2, 0))[..., None])
    dscore_b = dscore.astype(jnp.bfloat16).astype(jnp.float32)
    query_grad = (jnp.einsum('grqk,kgd->qgrd', dscore_b, key_f) * score_scale).astype(jnp.bfloat16)
    key_grad = (jnp.einsum('grqk,qgrd->kgd', dscore_b, query_f) * score_scale).astype(jnp.bfloat16)
    value_grad = jnp.einsum('grqk,qgrd->kgd', probs_b, grad_f).astype(jnp.bfloat16)
    joined = jnp.concatenate([query_grad.reshape(length, KV_HEADS, GROUP * HEAD_DIM), key_grad, value_grad], axis=2)
    return joined.reshape(length, QKV_COLS)

def reference(layer_input, queries, keys_saved, values_saved, out_grad, master_weight, first_moment, second_moment):

    def per_sequence(running, seq_items):
        input_seq, query_seq, key_seq, value_seq, grad_seq = seq_items
        grouped = sequence_grads(query_seq, key_seq, value_seq, grad_seq)
        partial_value = jnp.dot(input_seq.T, grouped, preferred_element_type=jnp.float32).astype(jnp.bfloat16)
        return (running + partial_value.astype(jnp.float32), None)
    gradient, unused = lax.scan(per_sequence, jnp.zeros((D, QKV_COLS), jnp.float32), (layer_input, queries, keys_saved, values_saved, out_grad))
    first_new = beta_first * first_moment + (1.0 - beta_first) * gradient
    second_new = beta_second * second_moment + (1.0 - beta_second) * gradient * gradient
    corr_first = 1.0 - beta_first ** STEP
    corr_second = 1.0 - beta_second ** STEP
    direction = first_new / corr_first / (jnp.sqrt(second_new / corr_second) + adam_epsilon) + decay_rate * master_weight
    trust_ratio = jnp.sqrt(jnp.sum(master_weight * master_weight)) / jnp.sqrt(jnp.sum(direction * direction))
    lamb_update = trust_ratio * direction
    new_weights = (master_weight - learn_rate * lamb_update).astype(jnp.bfloat16)
    return (first_new, second_new, lamb_update, new_weights)
```

```python
import functools

import jax
import jax.numpy as jnp
from jax import lax
from jax.experimental import pallas as pl
from jax.experimental.pallas import tpu as pltpu
from jax.sharding import PartitionSpec as P

HEAD_DIM = 128
STEP = 100


beta_first = 0.9
beta_second = 0.999
adam_epsilon = 1e-06
decay_rate = 0.01
learn_rate = 0.01
masked_score = -1e30

MESH_ID = pl.DeviceIdType.MESH
SLOW = 4


def nt(left, right):
    return lax.dot_general(
        left, right, (((1,), (1,)), ((), ())), preferred_element_type=jnp.float32
    )


def nn(left, right):
    return jnp.dot(left, right, preferred_element_type=jnp.float32)


def head_kernel(group, block, q_ref, k_ref, v_ref, g_ref, out_ref, dk_acc, dv_acc):
    head = pl.program_id(1)
    length = q_ref.shape[0]
    scale = HEAD_DIM ** (-0.5)

    @pl.when(head == 0)
    def _():
        dk_acc[...] = jnp.zeros_like(dk_acc)
        dv_acc[...] = jnp.zeros_like(dv_acc)

    for start in range(0, length, block):
        keys = start + block
        query = q_ref[start:keys, :]
        grad = g_ref[start:keys, :]
        key = k_ref[:keys, :]
        value = v_ref[:keys, :]
        scores = nt(key, query) * scale
        row = lax.broadcasted_iota(jnp.int32, (keys, block), 0)
        column = lax.broadcasted_iota(jnp.int32, (keys, block), 1) + start
        scores = jnp.where(row <= column, scores, masked_score)
        weights = jnp.exp(scores - jnp.max(scores, axis=0, keepdims=True))
        probs = weights / jnp.sum(weights, axis=0, keepdims=True)
        probs_b = probs.astype(jnp.bfloat16)
        prob_grad = nt(value, grad)
        row_delta = jnp.sum(probs_b.astype(jnp.float32) * prob_grad, axis=0, keepdims=True)
        dscore = (probs * (prob_grad - row_delta)).astype(jnp.bfloat16)
        dq = lax.dot_general(
            dscore, key, (((0,), (0,)), ((), ())), preferred_element_type=jnp.float32
        )
        column_start = pl.multiple_of(head * HEAD_DIM, HEAD_DIM)
        out_ref[start:keys, pl.ds(column_start, HEAD_DIM)] = (dq * scale).astype(jnp.bfloat16)
        dk_acc[:keys, :] += nn(dscore, query)
        dv_acc[:keys, :] += nn(probs_b, grad)

    @pl.when(head == group - 1)
    def _():
        width = group * HEAD_DIM
        out_ref[:, width : width + HEAD_DIM] = (dk_acc[...] * scale).astype(jnp.bfloat16)
        out_ref[:, width + HEAD_DIM :] = dv_acc[...].astype(jnp.bfloat16)


def head_grads(query, key, value, grad):
    length = query.shape[0]
    kv_local = key.shape[1] // HEAD_DIM
    group = query.shape[1] // key.shape[1]
    query_spec = pl.BlockSpec((length, HEAD_DIM), lambda g, h: (0, g * group + h))
    key_spec = pl.BlockSpec((length, HEAD_DIM), lambda g, h: (0, g))
    return pl.pallas_call(
        functools.partial(head_kernel, group, min(256, length)),
        grid=(kv_local, group),
        in_specs=[query_spec, key_spec, key_spec, query_spec],
        out_specs=pl.BlockSpec((length, (group + 2) * HEAD_DIM), lambda g, h: (0, g)),
        out_shape=jax.ShapeDtypeStruct(
            (length, kv_local * (group + 2) * HEAD_DIM), jnp.bfloat16
        ),
        scratch_shapes=[pltpu.VMEM((length, HEAD_DIM), jnp.float32)] * 2,
        compiler_params=pltpu.CompilerParams(vmem_limit_bytes=40 * 1024 * 1024),
        cost_estimate=pl.CostEstimate(
            flops=10 * length * length * query.shape[1],
            bytes_accessed=8 * length * query.shape[1],
            transcendentals=length * length * kv_local * group,
        ),
        name="head_grads",
    )(query, key, value, grad)


def gather_kernel(slow, fast, chunks, tail, x_ref, out_ref, *sems):
    local_sem, p1s, p1r, x1s, x1r, x2s, x2r, p2s, p2r = sems
    me = lax.axis_index("dp")
    a = me // fast
    b = lax.rem(me, fast)
    lines = {"a": (a, slow, fast), "b": (b, fast, 1)}
    n_chunks = len(chunks)

    def neighbour(line, way):
        return me + way * lines[line][2]

    def can(line, way):
        pos, size, _ = lines[line]
        return pos + 1 < size if way > 0 else pos > 0

    barrier = pltpu.get_barrier_semaphore()
    for line in ("a", "b"):
        for way in (1, -1):

            @pl.when(can(line, way))
            def _(line=line, way=way):
                pl.semaphore_signal(
                    barrier,
                    inc=1,
                    device_id={"dp": neighbour(line, way)},
                    device_id_type=MESH_ID,
                )

    neighbours = sum(
        can(line, way).astype(jnp.int32) for line in ("a", "b") for way in (1, -1)
    )
    pl.semaphore_wait(barrier, neighbours)

    local = pltpu.make_async_copy(x_ref, out_ref.at[me], local_sem)
    local.start()

    def piece(origin, rows, own):
        start, size = rows
        if own:
            return x_ref.at[pl.ds(start, size)]
        return out_ref.at[origin, pl.ds(start, size)]

    def copy(line, way, origin, rows, own, send, recv):
        start, size = rows
        return pltpu.make_async_remote_copy(
            src_ref=piece(origin, rows, own),
            dst_ref=out_ref.at[origin, pl.ds(start, size)],
            send_sem=send,
            recv_sem=recv,
            device_id={"dp": neighbour(line, way)},
            device_id_type=MESH_ID,
        )

    pending = []

    def send(condition, *args):
        @pl.when(condition)
        def _():
            copy(*args).start()

        pending.append((condition, args))

    def both(first, second):
        return jnp.logical_and(first, second)

    def send_a1(step, c, way):
        origin_a = a - way * step
        inside = origin_a >= 0 if way > 0 else origin_a < slow
        d = 0 if way > 0 else 1
        i = (d * (slow - 1) + step) * n_chunks + c
        send(
            both(can("a", way), inside),
            "a", way, origin_a * fast + b, chunks[c], step == 0, p1s.at[i], p1r.at[i],
        )

    def recv_a1(step, c, way):
        origin_a = a - way * (step + 1)
        inside = origin_a >= 0 if way > 0 else origin_a < slow
        d = 0 if way > 0 else 1
        i = (d * (slow - 1) + step) * n_chunks + c

        @pl.when(inside)
        def _():
            copy("a", -way, origin_a * fast + b, chunks[c], False, p1s.at[i], p1r.at[i]).wait_recv()

        return inside, origin_a

    def send_b1(step, slot, c, way, present):
        origin_a = a + slot
        origin_b = b - way * step
        inside = origin_b >= 0 if way > 0 else origin_b < fast
        d = 0 if way > 0 else 1
        i = ((d * (fast - 1) + step) * (2 * slow - 1) + slot + slow - 1) * n_chunks + c
        send(
            both(present, both(can("b", way), inside)),
            "b", way, origin_a * fast + origin_b, chunks[c], step == 0 and slot == 0,
            x1s.at[i], x1r.at[i],
        )

    def recv_b1(step, slot, c, way):
        origin_a = a + slot
        present = both(origin_a >= 0, origin_a < slow)
        origin_b = b - way * (step + 1)
        inside = origin_b >= 0 if way > 0 else origin_b < fast
        d = 0 if way > 0 else 1
        i = ((d * (fast - 1) + step) * (2 * slow - 1) + slot + slow - 1) * n_chunks + c

        @pl.when(both(present, inside))
        def _():
            copy(
                "b", -way, origin_a * fast + origin_b, chunks[c], False, x1s.at[i], x1r.at[i]
            ).wait_recv()

        return present

    def send_b2(step, way):
        origin_b = b - way * step
        inside = origin_b >= 0 if way > 0 else origin_b < fast
        i = (0 if way > 0 else 1) * (fast - 1) + step
        send(
            both(can("b", way), inside),
            "b", way, a * fast + origin_b, tail, step == 0, x2s.at[i], x2r.at[i],
        )

    def recv_b2(step, way):
        origin_b = b - way * (step + 1)
        inside = origin_b >= 0 if way > 0 else origin_b < fast
        i = (0 if way > 0 else 1) * (fast - 1) + step

        @pl.when(inside)
        def _():
            copy("b", -way, a * fast + origin_b, tail, False, x2s.at[i], x2r.at[i]).wait_recv()

        return inside

    def send_a2(step, turn, way):
        origin_a = a - way * step
        inside = origin_a >= 0 if way > 0 else origin_a < slow
        origin_b = lax.rem(b + turn, fast)
        i = ((0 if way > 0 else 1) * (slow - 1) + step) * fast + turn
        send(
            both(can("a", way), inside),
            "a", way, origin_a * fast + origin_b, tail, step == 0 and turn == 0,
            p2s.at[i], p2r.at[i],
        )

    def recv_a2(step, turn, way):
        origin_a = a - way * (step + 1)
        inside = origin_a >= 0 if way > 0 else origin_a < slow
        origin_b = lax.rem(b + turn, fast)
        i = ((0 if way > 0 else 1) * (slow - 1) + step) * fast + turn

        @pl.when(inside)
        def _():
            copy(
                "a", -way, origin_a * fast + origin_b, tail, False, p2s.at[i], p2r.at[i]
            ).wait_recv()

    ways = (1, -1)
    always = a >= 0
    for c in range(n_chunks):
        for way in ways:
            send_a1(0, c, way)
        for way in ways:
            send_b1(0, 0, c, way, always)
    for way in ways:
        send_b2(0, way)
    for way in ways:
        send_a2(0, 0, way)
    for step in range(slow - 1):
        for c in range(n_chunks):
            for way in ways:
                present, _ = recv_a1(step, c, way)
                if step + 1 < slow - 1:
                    send_a1(step + 1, c, way)
                for way_b in ways:
                    send_b1(0, -way * (step + 1), c, way_b, present)
        if step == 0:
            for hop in range(fast - 1):
                for way in ways:
                    recv_b2(hop, way)
                    if hop + 1 < fast - 1:
                        send_b2(hop + 1, way)
            for turn in range(1, fast):
                for way in ways:
                    send_a2(0, turn, way)
        for turn in range(fast):
            for way in ways:
                recv_a2(step, turn, way)
                if step + 1 < slow - 1:
                    send_a2(step + 1, turn, way)
    slots = [0] + [sign * far for far in range(1, slow) for sign in (-1, 1)]
    for hop in range(fast - 1):
        for slot in slots:
            for c in range(n_chunks):
                for way in ways:
                    present = recv_b1(hop, slot, c, way)
                    if hop + 1 < fast - 1:
                        send_b1(hop + 1, slot, c, way, present)
    local.wait()
    for condition, args in pending:

        @pl.when(condition)
        def _(args=args):
            copy(*args).wait_send()


def gather_dp(shard, devices, collective_id, name):
    rows, columns = shard.shape
    slow = SLOW
    fast = devices // SLOW
    first = rows * 13 // 16 // 32 * 32
    chunks = ((0, first // 2), (first // 2, first // 2))
    tail = (first, rows - first)
    n_chunks = len(chunks)
    dma = pltpu.SemaphoreType.DMA
    sizes = (
        2 * (slow - 1) * n_chunks,
        2 * (fast - 1) * (2 * slow - 1) * n_chunks,
        2 * (fast - 1),
        2 * (slow - 1) * fast,
    )
    return pl.pallas_call(
        functools.partial(gather_kernel, slow, fast, chunks, tail),
        in_specs=[pl.BlockSpec(memory_space=pl.ANY)],
        out_specs=pl.BlockSpec(memory_space=pl.ANY),
        out_shape=jax.ShapeDtypeStruct((devices, rows, columns), shard.dtype),
        scratch_shapes=[dma] + [dma((size,)) for size in sizes for _ in range(2)],
        compiler_params=pltpu.CompilerParams(
            collective_id=collective_id, has_side_effects=True
        ),
        cost_estimate=pl.CostEstimate(
            flops=0, bytes_accessed=4 * devices * rows * columns, transcendentals=0
        ),
        name=name,
    )(shard)


def body(
    devices,
    layer_input,
    queries,
    keys_saved,
    values_saved,
    out_grad,
    master_weight,
    first_moment,
    second_moment,
):
    weight_sq = jnp.sum(master_weight * master_weight)
    input_rows = lax.all_to_all(layer_input, "dp", split_axis=2, concat_axis=0, tiled=True)
    input_rows = lax.all_gather(input_rows, "ctx", axis=1, tiled=True)
    query_heads, key_heads, value_heads, grad_heads = (
        lax.all_to_all(queries, "ctx", split_axis=2, concat_axis=1, tiled=True),
        lax.all_to_all(keys_saved, "ctx", split_axis=2, concat_axis=1, tiled=True),
        lax.all_to_all(values_saved, "ctx", split_axis=2, concat_axis=1, tiled=True),
        lax.all_to_all(out_grad, "ctx", split_axis=2, concat_axis=1, tiled=True),
    )
    grouped = head_grads(query_heads[0], key_heads[0], value_heads[0], grad_heads[0])
    grouped_all = gather_dp(grouped, devices, 1, "gather_grouped")
    gradient = lax.dot_general(
        input_rows,
        grouped_all,
        (((0, 1), (0, 1)), ((), ())),
        preferred_element_type=jnp.float32,
    )
    first_new = beta_first * first_moment + (1.0 - beta_first) * gradient
    second_new = beta_second * second_moment + (1.0 - beta_second) * gradient * gradient
    corr_first = 1.0 - beta_first**STEP
    corr_second = 1.0 - beta_second**STEP
    direction = (
        first_new / corr_first / (jnp.sqrt(second_new / corr_second) + adam_epsilon)
        + decay_rate * master_weight
    )
    update_sq = jnp.sum(direction * direction)
    weight_total, update_total = lax.psum((weight_sq, update_sq), ("dp", "ctx"))
    trust_ratio = jnp.sqrt(weight_total) / jnp.sqrt(update_total)
    lamb_update = trust_ratio * direction
    new_local = (master_weight - learn_rate * lamb_update).astype(jnp.bfloat16)
    new_weights = gather_dp(new_local, devices, 2, "gather_weights")
    return (first_new, second_new, lamb_update, new_weights.reshape(-1, new_local.shape[1]))


def solution(mesh):
    in_specs = (
        P("dp", "ctx", None),
        P("dp", "ctx", None),
        P("dp", "ctx", None),
        P("dp", "ctx", None),
        P("dp", "ctx", None),
        P("dp", "ctx"),
        P("dp", "ctx"),
        P("dp", "ctx"),
    )
    out_specs = (P("dp", "ctx"), P("dp", "ctx"), P("dp", "ctx"), P(None, "ctx"))
    return jax.shard_map(
        functools.partial(body, mesh.shape["dp"]),
        mesh=mesh,
        in_specs=in_specs,
        out_specs=out_specs,
        check_vma=False,
    )
```

```python
import functools

import jax
import jax.numpy as jnp
from jax import lax
from jax.experimental import pallas as pl
from jax.experimental.pallas import tpu as pltpu
from jax.sharding import PartitionSpec as P

HEAD_DIM = 128
STEP = 100


beta_first = 0.9
beta_second = 0.999
adam_epsilon = 1e-06
decay_rate = 0.01
learn_rate = 0.01
masked_score = -1e30

MESH_ID = pl.DeviceIdType.MESH
SLOW = 4


def nt(left, right):
    return lax.dot_general(
        left, right, (((1,), (1,)), ((), ())), preferred_element_type=jnp.float32
    )


def nn(left, right):
    return jnp.dot(left, right, preferred_element_type=jnp.float32)


def head_kernel(group, block, q_ref, k_ref, v_ref, g_ref, out_ref, dk_acc, dv_acc):
    head = pl.program_id(1)
    length = q_ref.shape[0]
    scale = HEAD_DIM ** (-0.5)

    @pl.when(head == 0)
    def _():
        dk_acc[...] = jnp.zeros_like(dk_acc)
        dv_acc[...] = jnp.zeros_like(dv_acc)

    for start in range(0, length, block):
        keys = start + block
        query = q_ref[start:keys, :]
        grad = g_ref[start:keys, :]
        key = k_ref[:keys, :]
        value = v_ref[:keys, :]
        scores = nt(key, query) * scale
        row = lax.broadcasted_iota(jnp.int32, (keys, block), 0)
        column = lax.broadcasted_iota(jnp.int32, (keys, block), 1) + start
        scores = jnp.where(row <= column, scores, masked_score)
        weights = jnp.exp(scores - jnp.max(scores, axis=0, keepdims=True))
        probs = weights / jnp.sum(weights, axis=0, keepdims=True)
        probs_b = probs.astype(jnp.bfloat16)
        prob_grad = nt(value, grad)
        row_delta = jnp.sum(probs_b.astype(jnp.float32) * prob_grad, axis=0, keepdims=True)
        dscore = (probs * (prob_grad - row_delta)).astype(jnp.bfloat16)
        dq = lax.dot_general(
            dscore, key, (((0,), (0,)), ((), ())), preferred_element_type=jnp.float32
        )
        column_start = pl.multiple_of(head * HEAD_DIM, HEAD_DIM)
        out_ref[start:keys, pl.ds(column_start, HEAD_DIM)] = (dq * scale).astype(jnp.bfloat16)
        dk_acc[:keys, :] += nn(dscore, query)
        dv_acc[:keys, :] += nn(probs_b, grad)

    @pl.when(head == group - 1)
    def _():
        width = group * HEAD_DIM
        out_ref[:, width : width + HEAD_DIM] = (dk_acc[...] * scale).astype(jnp.bfloat16)
        out_ref[:, width + HEAD_DIM :] = dv_acc[...].astype(jnp.bfloat16)


def head_grads(query, key, value, grad):
    length = query.shape[0]
    kv_local = key.shape[1] // HEAD_DIM
    group = query.shape[1] // key.shape[1]
    query_spec = pl.BlockSpec((length, HEAD_DIM), lambda g, h: (0, g * group + h))
    key_spec = pl.BlockSpec((length, HEAD_DIM), lambda g, h: (0, g))
    return pl.pallas_call(
        functools.partial(head_kernel, group, min(256, length)),
        grid=(kv_local, group),
        in_specs=[query_spec, key_spec, key_spec, query_spec],
        out_specs=pl.BlockSpec((length, (group + 2) * HEAD_DIM), lambda g, h: (0, g)),
        out_shape=jax.ShapeDtypeStruct(
            (length, kv_local * (group + 2) * HEAD_DIM), jnp.bfloat16
        ),
        scratch_shapes=[pltpu.VMEM((length, HEAD_DIM), jnp.float32)] * 2,
        compiler_params=pltpu.CompilerParams(vmem_limit_bytes=40 * 1024 * 1024),
        cost_estimate=pl.CostEstimate(
            flops=10 * length * length * query.shape[1],
            bytes_accessed=8 * length * query.shape[1],
            transcendentals=length * length * kv_local * group,
        ),
        name="head_grads",
    )(query, key, value, grad)


def gather_kernel(slow, fast, chunks, tail, x_ref, out_ref, *sems):
    local_sem, p1s, p1r, x1s, x1r, x2s, x2r, p2s, p2r = sems
    me = lax.axis_index("dp")
    a = me // fast
    b = lax.rem(me, fast)
    lines = {"a": (a, slow, fast), "b": (b, fast, 1)}
    n_chunks = len(chunks)

    def neighbour(line, way):
        return me + way * lines[line][2]

    def can(line, way):
        pos, size, _ = lines[line]
        return pos + 1 < size if way > 0 else pos > 0

    barrier = pltpu.get_barrier_semaphore()
    for line in ("a", "b"):
        for way in (1, -1):

            @pl.when(can(line, way))
            def _(line=line, way=way):
                pl.semaphore_signal(
                    barrier,
                    inc=1,
                    device_id={"dp": neighbour(line, way)},
                    device_id_type=MESH_ID,
                )

    neighbours = sum(
        can(line, way).astype(jnp.int32) for line in ("a", "b") for way in (1, -1)
    )
    pl.semaphore_wait(barrier, neighbours)

    local = pltpu.make_async_copy(x_ref, out_ref.at[me], local_sem)
    local.start()

    def piece(origin, rows, own):
        start, size = rows
        if own:
            return x_ref.at[pl.ds(start, size)]
        return out_ref.at[origin, pl.ds(start, size)]

    def copy(line, way, origin, rows, own, send, recv):
        start, size = rows
        return pltpu.make_async_remote_copy(
            src_ref=piece(origin, rows, own),
            dst_ref=out_ref.at[origin, pl.ds(start, size)],
            send_sem=send,
            recv_sem=recv,
            device_id={"dp": neighbour(line, way)},
            device_id_type=MESH_ID,
        )

    pending = []

    def send(condition, *args):
        @pl.when(condition)
        def _():
            copy(*args).start()

        pending.append((condition, args))

    def both(first, second):
        return jnp.logical_and(first, second)

    def send_a1(step, c, way):
        origin_a = a - way * step
        inside = origin_a >= 0 if way > 0 else origin_a < slow
        d = 0 if way > 0 else 1
        i = (d * (slow - 1) + step) * n_chunks + c
        send(
            both(can("a", way), inside),
            "a", way, origin_a * fast + b, chunks[c], step == 0, p1s.at[i], p1r.at[i],
        )

    def recv_a1(step, c, way):
        origin_a = a - way * (step + 1)
        inside = origin_a >= 0 if way > 0 else origin_a < slow
        d = 0 if way > 0 else 1
        i = (d * (slow - 1) + step) * n_chunks + c

        @pl.when(inside)
        def _():
            copy("a", -way, origin_a * fast + b, chunks[c], False, p1s.at[i], p1r.at[i]).wait_recv()

        return inside, origin_a

    def send_b1(step, slot, c, way, present):
        origin_a = a + slot
        origin_b = b - way * step
        inside = origin_b >= 0 if way > 0 else origin_b < fast
        d = 0 if way > 0 else 1
        i = ((d * (fast - 1) + step) * (2 * slow - 1) + slot + slow - 1) * n_chunks + c
        send(
            both(present, both(can("b", way), inside)),
            "b", way, origin_a * fast + origin_b, chunks[c], step == 0 and slot == 0,
            x1s.at[i], x1r.at[i],
        )

    def recv_b1(step, slot, c, way):
        origin_a = a + slot
        present = both(origin_a >= 0, origin_a < slow)
        origin_b = b - way * (step + 1)
        inside = origin_b >= 0 if way > 0 else origin_b < fast
        d = 0 if way > 0 else 1
        i = ((d * (fast - 1) + step) * (2 * slow - 1) + slot + slow - 1) * n_chunks + c

        @pl.when(both(present, inside))
        def _():
            copy(
                "b", -way, origin_a * fast + origin_b, chunks[c], False, x1s.at[i], x1r.at[i]
            ).wait_recv()

        return present

    def send_b2(step, way):
        origin_b = b - way * step
        inside = origin_b >= 0 if way > 0 else origin_b < fast
        i = (0 if way > 0 else 1) * (fast - 1) + step
        send(
            both(can("b", way), inside),
            "b", way, a * fast + origin_b, tail, step == 0, x2s.at[i], x2r.at[i],
        )

    def recv_b2(step, way):
        origin_b = b - way * (step + 1)
        inside = origin_b >= 0 if way > 0 else origin_b < fast
        i = (0 if way > 0 else 1) * (fast - 1) + step

        @pl.when(inside)
        def _():
            copy("b", -way, a * fast + origin_b, tail, False, x2s.at[i], x2r.at[i]).wait_recv()

        return inside

    def send_a2(step, turn, way):
        origin_a = a - way * step
        inside = origin_a >= 0 if way > 0 else origin_a < slow
        origin_b = lax.rem(b + turn, fast)
        i = ((0 if way > 0 else 1) * (slow - 1) + step) * fast + turn
        send(
            both(can("a", way), inside),
            "a", way, origin_a * fast + origin_b, tail, step == 0 and turn == 0,
            p2s.at[i], p2r.at[i],
        )

    def recv_a2(step, turn, way):
        origin_a = a - way * (step + 1)
        inside = origin_a >= 0 if way > 0 else origin_a < slow
        origin_b = lax.rem(b + turn, fast)
        i = ((0 if way > 0 else 1) * (slow - 1) + step) * fast + turn

        @pl.when(inside)
        def _():
            copy(
                "a", -way, origin_a * fast + origin_b, tail, False, p2s.at[i], p2r.at[i]
            ).wait_recv()

    ways = (1, -1)
    always = a >= 0
    for c in range(n_chunks):
        for way in ways:
            send_a1(0, c, way)
        for way in ways:
            send_b1(0, 0, c, way, always)
    for way in ways:
        send_b2(0, way)
    for way in ways:
        send_a2(0, 0, way)
    for step in range(slow - 1):
        for c in range(n_chunks):
            for way in ways:
                present, _ = recv_a1(step, c, way)
                if step + 1 < slow - 1:
                    send_a1(step + 1, c, way)
                for way_b in ways:
                    send_b1(0, -way * (step + 1), c, way_b, present)
        if step == 0:
            for hop in range(fast - 1):
                for way in ways:
                    recv_b2(hop, way)
                    if hop + 1 < fast - 1:
                        send_b2(hop + 1, way)
            for turn in range(1, fast):
                for way in ways:
                    send_a2(0, turn, way)
        for turn in range(fast):
            for way in ways:
                recv_a2(step, turn, way)
                if step + 1 < slow - 1:
                    send_a2(step + 1, turn, way)
    slots = [0] + [sign * far for far in range(1, slow) for sign in (-1, 1)]
    for hop in range(fast - 1):
        for slot in slots:
            for c in range(n_chunks):
                for way in ways:
                    present = recv_b1(hop, slot, c, way)
                    if hop + 1 < fast - 1:
                        send_b1(hop + 1, slot, c, way, present)
    local.wait()
    for condition, args in pending:

        @pl.when(condition)
        def _(args=args):
            copy(*args).wait_send()


def gather_dp(shard, devices, collective_id, name):
    rows, columns = shard.shape
    slow = SLOW
    fast = devices // SLOW
    first = rows * 13 // 16 // 32 * 32
    chunks = ((0, first // 2), (first // 2, first // 2))
    tail = (first, rows - first)
    n_chunks = len(chunks)
    dma = pltpu.SemaphoreType.DMA
    sizes = (
        2 * (slow - 1) * n_chunks,
        2 * (fast - 1) * (2 * slow - 1) * n_chunks,
        2 * (fast - 1),
        2 * (slow - 1) * fast,
    )
    return pl.pallas_call(
        functools.partial(gather_kernel, slow, fast, chunks, tail),
        in_specs=[pl.BlockSpec(memory_space=pl.ANY)],
        out_specs=pl.BlockSpec(memory_space=pl.ANY),
        out_shape=jax.ShapeDtypeStruct((devices, rows, columns), shard.dtype),
        scratch_shapes=[dma] + [dma((size,)) for size in sizes for _ in range(2)],
        compiler_params=pltpu.CompilerParams(
            collective_id=collective_id, has_side_effects=True
        ),
        cost_estimate=pl.CostEstimate(
            flops=0, bytes_accessed=4 * devices * rows * columns, transcendentals=0
        ),
        name=name,
    )(shard)


def exchange_kernel(n_ctx, n_dp, widths, input_width, *refs):
    count = len(widths)
    sources, source_input = refs[:count], refs[count]
    targets, target_input = refs[count + 1 : 2 * count + 1], refs[2 * count + 1]
    ctx_send, ctx_recv, dp_send, dp_recv, local_sems = refs[2 * count + 2 :]
    dp = lax.axis_index("dp")
    ctx = lax.axis_index("ctx")
    rows = source_input.shape[0]
    barrier = pltpu.get_barrier_semaphore()
    for turn in range(1, n_ctx):
        pl.semaphore_signal(
            barrier, inc=1, device_id={"ctx": lax.rem(ctx + turn, n_ctx)}, device_id_type=MESH_ID
        )
    for turn in range(1, n_dp):
        pl.semaphore_signal(
            barrier, inc=1, device_id={"dp": lax.rem(dp + turn, n_dp)}, device_id_type=MESH_ID
        )
    pl.semaphore_wait(barrier, n_ctx + n_dp - 2)

    def source(i, peer):
        return sources[i].at[:, pl.ds(pl.multiple_of(peer * widths[i], 128), widths[i])]

    def source_columns(peer):
        return source_input.at[:, pl.ds(pl.multiple_of(peer * input_width, 128), input_width)]

    def row_block(i, owner):
        return targets[i].at[pl.ds(pl.multiple_of(owner * rows, 16), rows)]

    copies = []
    for turn in range(1, n_ctx):
        peer = lax.rem(ctx + turn, n_ctx)
        for i in range(count):
            k = i * (n_ctx - 1) + turn - 1
            copies.append(
                pltpu.make_async_remote_copy(
                    src_ref=source(i, peer),
                    dst_ref=row_block(i, ctx),
                    send_sem=ctx_send.at[k],
                    recv_sem=ctx_recv.at[k],
                    device_id={"ctx": peer},
                    device_id_type=MESH_ID,
                )
            )
            copies[-1].start()
    for turn in range(1, n_dp):
        peer = lax.rem(dp + turn, n_dp)
        copies.append(
            pltpu.make_async_remote_copy(
                src_ref=source_columns(peer),
                dst_ref=target_input.at[dp],
                send_sem=dp_send.at[turn - 1],
                recv_sem=dp_recv.at[turn - 1],
                device_id={"dp": peer},
                device_id_type=MESH_ID,
            )
        )
        copies[-1].start()
    owns = [
        pltpu.make_async_copy(source(i, ctx), row_block(i, ctx), local_sems.at[i])
        for i in range(count)
    ]
    owns.append(
        pltpu.make_async_copy(source_columns(dp), target_input.at[dp], local_sems.at[count])
    )
    for own in owns:
        own.start()
    for own in owns:
        own.wait()
    for turn in range(1, n_ctx):
        origin = lax.rem(ctx + n_ctx - turn, n_ctx)
        for i in range(count):
            k = i * (n_ctx - 1) + turn - 1
            pltpu.make_async_remote_copy(
                src_ref=source(i, origin),
                dst_ref=row_block(i, origin),
                send_sem=ctx_send.at[k],
                recv_sem=ctx_recv.at[k],
                device_id={"ctx": origin},
                device_id_type=MESH_ID,
            ).wait_recv()
    for turn in range(1, n_dp):
        origin = lax.rem(dp + n_dp - turn, n_dp)
        pltpu.make_async_remote_copy(
            src_ref=source_columns(origin),
            dst_ref=target_input.at[origin],
            send_sem=dp_send.at[turn - 1],
            recv_sem=dp_recv.at[turn - 1],
            device_id={"dp": origin},
            device_id_type=MESH_ID,
        ).wait_recv()
    for copy in copies:
        copy.wait_send()


def exchange(arrays, layer_input, n_ctx, n_dp):
    rows = layer_input.shape[0]
    widths = tuple(array.shape[1] // n_ctx for array in arrays)
    input_width = layer_input.shape[1] // n_dp
    dma = pltpu.SemaphoreType.DMA
    ctx_copies = len(arrays) * (n_ctx - 1)
    anywhere = pl.BlockSpec(memory_space=pl.ANY)
    return pl.pallas_call(
        functools.partial(exchange_kernel, n_ctx, n_dp, widths, input_width),
        in_specs=[anywhere] * (len(arrays) + 1),
        out_specs=[anywhere] * (len(arrays) + 1),
        out_shape=[
            jax.ShapeDtypeStruct((rows * n_ctx, width), jnp.bfloat16) for width in widths
        ]
        + [jax.ShapeDtypeStruct((n_dp, rows, input_width), jnp.bfloat16)],
        scratch_shapes=[
            dma((ctx_copies,)),
            dma((ctx_copies,)),
            dma((n_dp - 1,)),
            dma((n_dp - 1,)),
            dma((len(arrays) + 1,)),
        ],
        compiler_params=pltpu.CompilerParams(collective_id=3, has_side_effects=True),
        cost_estimate=pl.CostEstimate(
            flops=0, bytes_accessed=8 * rows * layer_input.shape[1], transcendentals=0
        ),
        name="exchange",
    )(*arrays, layer_input)


def total_kernel(n_ctx, n_dp, x_ref, out_ref, held_dp, part, held_ctx, *sems):
    dp_send, dp_recv, ctx_send, ctx_recv = sems
    dp = lax.axis_index("dp")
    ctx = lax.axis_index("ctx")
    stages = (
        ("dp", dp, n_dp, x_ref, held_dp, dp_send, dp_recv),
        ("ctx", ctx, n_ctx, part, held_ctx, ctx_send, ctx_recv),
    )
    barrier = pltpu.get_barrier_semaphore()
    for axis, me, size, *_ in stages:
        for turn in range(1, size):
            pl.semaphore_signal(
                barrier, inc=1, device_id={axis: lax.rem(me + turn, size)}, device_id_type=MESH_ID
            )
    pl.semaphore_wait(barrier, n_ctx + n_dp - 2)
    for axis, me, size, block, held, send, recv in stages:
        copies = [
            pltpu.make_async_remote_copy(
                src_ref=block,
                dst_ref=held.at[turn - 1],
                send_sem=send.at[turn - 1],
                recv_sem=recv.at[turn - 1],
                device_id={axis: lax.rem(me + turn, size)},
                device_id_type=MESH_ID,
            )
            for turn in range(1, size)
        ]
        for copy in copies:
            copy.start()
        for copy in copies:
            copy.wait()
        total = block[...]
        for turn in range(1, size):
            total += held[turn - 1]
        if axis == "dp":
            part[...] = total
        else:
            out_ref[...] = total


def total_over_devices(first, second, n_ctx, n_dp):
    rows = jnp.arange(8)[:, None]
    block = jnp.where(rows == 0, first, jnp.where(rows == 1, second, 0.0))
    block = jnp.broadcast_to(block, (8, 128)).astype(jnp.float32)
    dma = pltpu.SemaphoreType.DMA
    total = pl.pallas_call(
        functools.partial(total_kernel, n_ctx, n_dp),
        in_specs=[pl.BlockSpec(memory_space=pltpu.VMEM)],
        out_specs=pl.BlockSpec(memory_space=pltpu.VMEM),
        out_shape=jax.ShapeDtypeStruct((8, 128), jnp.float32),
        scratch_shapes=[
            pltpu.VMEM((n_dp - 1, 8, 128), jnp.float32),
            pltpu.VMEM((8, 128), jnp.float32),
            pltpu.VMEM((n_ctx - 1, 8, 128), jnp.float32),
            dma((n_dp - 1,)),
            dma((n_dp - 1,)),
            dma((n_ctx - 1,)),
            dma((n_ctx - 1,)),
        ],
        compiler_params=pltpu.CompilerParams(collective_id=4, has_side_effects=True),
        cost_estimate=pl.CostEstimate(flops=0, bytes_accessed=65536, transcendentals=0),
        name="total",
    )(block)
    return total[0, 0], total[1, 0]


def body(
    devices,
    heads_split,
    layer_input,
    queries,
    keys_saved,
    values_saved,
    out_grad,
    master_weight,
    first_moment,
    second_moment,
):
    weight_sq = jnp.sum(master_weight * master_weight)
    *heads, input_rows = exchange(
        (queries[0], keys_saved[0], values_saved[0], out_grad[0]),
        layer_input[0],
        heads_split,
        devices,
    )
    input_rows = lax.all_gather(input_rows, "ctx", axis=1, tiled=True)
    grouped = head_grads(*heads)
    grouped_all = gather_dp(grouped, devices, 1, "gather_grouped")
    gradient = lax.dot_general(
        input_rows,
        grouped_all,
        (((0, 1), (0, 1)), ((), ())),
        preferred_element_type=jnp.float32,
    )
    first_new = beta_first * first_moment + (1.0 - beta_first) * gradient
    second_new = beta_second * second_moment + (1.0 - beta_second) * gradient * gradient
    corr_first = 1.0 - beta_first**STEP
    corr_second = 1.0 - beta_second**STEP
    direction = (
        first_new / corr_first / (jnp.sqrt(second_new / corr_second) + adam_epsilon)
        + decay_rate * master_weight
    )
    update_sq = jnp.sum(direction * direction)
    weight_total, update_total = total_over_devices(
        weight_sq, update_sq, heads_split, devices
    )
    trust_ratio = jnp.sqrt(weight_total) / jnp.sqrt(update_total)
    lamb_update = trust_ratio * direction
    new_local = (master_weight - learn_rate * lamb_update).astype(jnp.bfloat16)
    new_weights = gather_dp(new_local, devices, 2, "gather_weights")
    return (first_new, second_new, lamb_update, new_weights.reshape(-1, new_local.shape[1]))


def solution(mesh):
    in_specs = (
        P("dp", "ctx", None),
        P("dp", "ctx", None),
        P("dp", "ctx", None),
        P("dp", "ctx", None),
        P("dp", "ctx", None),
        P("dp", "ctx"),
        P("dp", "ctx"),
        P("dp", "ctx"),
    )
    out_specs = (P("dp", "ctx"), P("dp", "ctx"), P("dp", "ctx"), P(None, "ctx"))
    return jax.shard_map(
        functools.partial(body, mesh.shape["dp"], mesh.shape["ctx"]),
        mesh=mesh,
        in_specs=in_specs,
        out_specs=out_specs,
        check_vma=False,
    )
```

```python
import functools

import jax
import jax.numpy as jnp
from jax import lax
from jax.experimental import pallas as pl
from jax.experimental.pallas import tpu as pltpu
from jax.sharding import PartitionSpec as P

HEAD_DIM = 128
STEP = 100


beta_first = 0.9
beta_second = 0.999
adam_epsilon = 1e-06
decay_rate = 0.01
learn_rate = 0.01
masked_score = -1e30

MESH_ID = pl.DeviceIdType.MESH
SLOW = 4


def nt(left, right):
    return lax.dot_general(
        left, right, (((1,), (1,)), ((), ())), preferred_element_type=jnp.float32
    )


def nn(left, right):
    return jnp.dot(left, right, preferred_element_type=jnp.float32)


def head_kernel(group, block, q_ref, k_ref, v_ref, g_ref, out_ref, dk_acc, dv_acc):
    head = pl.program_id(1)
    length = q_ref.shape[0]
    scale = HEAD_DIM ** (-0.5)

    @pl.when(head == 0)
    def _():
        dk_acc[...] = jnp.zeros_like(dk_acc)
        dv_acc[...] = jnp.zeros_like(dv_acc)

    for start in range(0, length, block):
        keys = start + block
        query = q_ref[start:keys, :]
        grad = g_ref[start:keys, :]
        key = k_ref[:keys, :]
        value = v_ref[:keys, :]
        scores = nt(key, query) * scale
        row = lax.broadcasted_iota(jnp.int32, (keys, block), 0)
        column = lax.broadcasted_iota(jnp.int32, (keys, block), 1) + start
        scores = jnp.where(row <= column, scores, masked_score)
        weights = jnp.exp(scores - jnp.max(scores, axis=0, keepdims=True))
        probs = weights / jnp.sum(weights, axis=0, keepdims=True)
        probs_b = probs.astype(jnp.bfloat16)
        prob_grad = nt(value, grad)
        row_delta = jnp.sum(probs_b.astype(jnp.float32) * prob_grad, axis=0, keepdims=True)
        dscore = (probs * (prob_grad - row_delta)).astype(jnp.bfloat16)
        dq = lax.dot_general(
            dscore, key, (((0,), (0,)), ((), ())), preferred_element_type=jnp.float32
        )
        column_start = pl.multiple_of(head * HEAD_DIM, HEAD_DIM)
        out_ref[start:keys, pl.ds(column_start, HEAD_DIM)] = (dq * scale).astype(jnp.bfloat16)
        dk_acc[:keys, :] += nn(dscore, query)
        dv_acc[:keys, :] += nn(probs_b, grad)

    @pl.when(head == group - 1)
    def _():
        width = group * HEAD_DIM
        out_ref[:, width : width + HEAD_DIM] = (dk_acc[...] * scale).astype(jnp.bfloat16)
        out_ref[:, width + HEAD_DIM :] = dv_acc[...].astype(jnp.bfloat16)


def head_grads(query, key, value, grad):
    length = query.shape[0]
    kv_local = key.shape[1] // HEAD_DIM
    group = query.shape[1] // key.shape[1]
    query_spec = pl.BlockSpec((length, HEAD_DIM), lambda g, h: (0, g * group + h))
    key_spec = pl.BlockSpec((length, HEAD_DIM), lambda g, h: (0, g))
    return pl.pallas_call(
        functools.partial(head_kernel, group, min(256, length)),
        grid=(kv_local, group),
        in_specs=[query_spec, key_spec, key_spec, query_spec],
        out_specs=pl.BlockSpec((length, (group + 2) * HEAD_DIM), lambda g, h: (0, g)),
        out_shape=jax.ShapeDtypeStruct(
            (length, kv_local * (group + 2) * HEAD_DIM), jnp.bfloat16
        ),
        scratch_shapes=[pltpu.VMEM((length, HEAD_DIM), jnp.float32)] * 2,
        compiler_params=pltpu.CompilerParams(vmem_limit_bytes=40 * 1024 * 1024),
        cost_estimate=pl.CostEstimate(
            flops=10 * length * length * query.shape[1],
            bytes_accessed=8 * length * query.shape[1],
            transcendentals=length * length * kv_local * group,
        ),
        name="head_grads",
    )(query, key, value, grad)


def gather_kernel(slow, fast, chunks, tail, x_ref, out_ref, *sems):
    local_sem, p1s, p1r, x1s, x1r, x2s, x2r, p2s, p2r = sems
    me = lax.axis_index("dp")
    a = me // fast
    b = lax.rem(me, fast)
    lines = {"a": (a, slow, fast), "b": (b, fast, 1)}
    n_chunks = len(chunks)

    def neighbour(line, way):
        return me + way * lines[line][2]

    def can(line, way):
        pos, size, _ = lines[line]
        return pos + 1 < size if way > 0 else pos > 0

    barrier = pltpu.get_barrier_semaphore()
    for line in ("a", "b"):
        for way in (1, -1):

            @pl.when(can(line, way))
            def _(line=line, way=way):
                pl.semaphore_signal(
                    barrier,
                    inc=1,
                    device_id={"dp": neighbour(line, way)},
                    device_id_type=MESH_ID,
                )

    neighbours = sum(
        can(line, way).astype(jnp.int32) for line in ("a", "b") for way in (1, -1)
    )
    pl.semaphore_wait(barrier, neighbours)

    local = pltpu.make_async_copy(x_ref, out_ref.at[me], local_sem)
    local.start()

    def piece(origin, rows, own):
        part = (pl.ds(*rows[:2]), pl.ds(*rows[2:]))
        if own:
            return x_ref.at[part]
        return out_ref.at[(origin, *part)]

    def copy(line, way, origin, rows, own, send, recv):
        return pltpu.make_async_remote_copy(
            src_ref=piece(origin, rows, own),
            dst_ref=piece(origin, rows, False),
            send_sem=send,
            recv_sem=recv,
            device_id={"dp": neighbour(line, way)},
            device_id_type=MESH_ID,
        )

    pending = []

    def send(condition, *args):
        @pl.when(condition)
        def _():
            copy(*args).start()

        pending.append((condition, args))

    def both(first, second):
        return jnp.logical_and(first, second)

    def send_a1(step, c, way):
        origin_a = a - way * step
        inside = origin_a >= 0 if way > 0 else origin_a < slow
        d = 0 if way > 0 else 1
        i = (d * (slow - 1) + step) * n_chunks + c
        send(
            both(can("a", way), inside),
            "a", way, origin_a * fast + b, chunks[c], step == 0, p1s.at[i], p1r.at[i],
        )

    def recv_a1(step, c, way):
        origin_a = a - way * (step + 1)
        inside = origin_a >= 0 if way > 0 else origin_a < slow
        d = 0 if way > 0 else 1
        i = (d * (slow - 1) + step) * n_chunks + c

        @pl.when(inside)
        def _():
            copy("a", -way, origin_a * fast + b, chunks[c], False, p1s.at[i], p1r.at[i]).wait_recv()

        return inside, origin_a

    def send_b1(step, slot, c, way, present):
        origin_a = a + slot
        origin_b = b - way * step
        inside = origin_b >= 0 if way > 0 else origin_b < fast
        d = 0 if way > 0 else 1
        i = ((d * (fast - 1) + step) * (2 * slow - 1) + slot + slow - 1) * n_chunks + c
        send(
            both(present, both(can("b", way), inside)),
            "b", way, origin_a * fast + origin_b, chunks[c], step == 0 and slot == 0,
            x1s.at[i], x1r.at[i],
        )

    def recv_b1(step, slot, c, way):
        origin_a = a + slot
        present = both(origin_a >= 0, origin_a < slow)
        origin_b = b - way * (step + 1)
        inside = origin_b >= 0 if way > 0 else origin_b < fast
        d = 0 if way > 0 else 1
        i = ((d * (fast - 1) + step) * (2 * slow - 1) + slot + slow - 1) * n_chunks + c

        @pl.when(both(present, inside))
        def _():
            copy(
                "b", -way, origin_a * fast + origin_b, chunks[c], False, x1s.at[i], x1r.at[i]
            ).wait_recv()

        return present

    def send_b2(step, way):
        origin_b = b - way * step
        inside = origin_b >= 0 if way > 0 else origin_b < fast
        i = (0 if way > 0 else 1) * (fast - 1) + step
        send(
            both(can("b", way), inside),
            "b", way, a * fast + origin_b, tail, step == 0, x2s.at[i], x2r.at[i],
        )

    def recv_b2(step, way):
        origin_b = b - way * (step + 1)
        inside = origin_b >= 0 if way > 0 else origin_b < fast
        i = (0 if way > 0 else 1) * (fast - 1) + step

        @pl.when(inside)
        def _():
            copy("b", -way, a * fast + origin_b, tail, False, x2s.at[i], x2r.at[i]).wait_recv()

        return inside

    def send_a2(step, turn, way):
        origin_a = a - way * step
        inside = origin_a >= 0 if way > 0 else origin_a < slow
        origin_b = lax.rem(b + turn, fast)
        i = ((0 if way > 0 else 1) * (slow - 1) + step) * fast + turn
        send(
            both(can("a", way), inside),
            "a", way, origin_a * fast + origin_b, tail, step == 0 and turn == 0,
            p2s.at[i], p2r.at[i],
        )

    def recv_a2(step, turn, way):
        origin_a = a - way * (step + 1)
        inside = origin_a >= 0 if way > 0 else origin_a < slow
        origin_b = lax.rem(b + turn, fast)
        i = ((0 if way > 0 else 1) * (slow - 1) + step) * fast + turn

        @pl.when(inside)
        def _():
            copy(
                "a", -way, origin_a * fast + origin_b, tail, False, p2s.at[i], p2r.at[i]
            ).wait_recv()

    ways = (1, -1)
    always = a >= 0
    for c in range(n_chunks):
        for way in ways:
            send_a1(0, c, way)
        for way in ways:
            send_b1(0, 0, c, way, always)
    for way in ways:
        send_b2(0, way)
    for step in range(slow - 1):
        for c in range(n_chunks):
            for way in ways:
                present, _ = recv_a1(step, c, way)
                if step + 1 < slow - 1:
                    send_a1(step + 1, c, way)
                for way_b in ways:
                    send_b1(0, -way * (step + 1), c, way_b, present)
    for way in ways:
        send_a2(0, 0, way)
    for hop in range(fast - 1):
        for way in ways:
            recv_b2(hop, way)
            if hop + 1 < fast - 1:
                send_b2(hop + 1, way)
    for turn in range(1, fast):
        for way in ways:
            send_a2(0, turn, way)
    for step in range(slow - 1):
        for turn in range(fast):
            for way in ways:
                recv_a2(step, turn, way)
                if step + 1 < slow - 1:
                    send_a2(step + 1, turn, way)
    slots = [0] + [sign * far for far in range(1, slow) for sign in (-1, 1)]
    for hop in range(fast - 1):
        for slot in slots:
            for c in range(n_chunks):
                for way in ways:
                    present = recv_b1(hop, slot, c, way)
                    if hop + 1 < fast - 1:
                        send_b1(hop + 1, slot, c, way, present)
    local.wait()
    for condition, args in pending:

        @pl.when(condition)
        def _(args=args):
            copy(*args).wait_send()


def gather_dp(shard, devices, collective_id, name):
    rows, columns = shard.shape
    slow = SLOW
    fast = devices // SLOW
    first = rows * 13 // 16 // 32 * 32
    half = first // 32 * 16
    wide = columns // 2
    chunks = tuple(
        (start, size, column, wide)
        for column in (0, wide)
        for start, size in ((0, half), (half, first - half))
    )
    tail = (first, rows - first, 0, columns)
    n_chunks = len(chunks)
    dma = pltpu.SemaphoreType.DMA
    sizes = (
        2 * (slow - 1) * n_chunks,
        2 * (fast - 1) * (2 * slow - 1) * n_chunks,
        2 * (fast - 1),
        2 * (slow - 1) * fast,
    )
    return pl.pallas_call(
        functools.partial(gather_kernel, slow, fast, chunks, tail),
        in_specs=[pl.BlockSpec(memory_space=pl.ANY)],
        out_specs=pl.BlockSpec(memory_space=pl.ANY),
        out_shape=jax.ShapeDtypeStruct((devices, rows, columns), shard.dtype),
        scratch_shapes=[dma] + [dma((size,)) for size in sizes for _ in range(2)],
        compiler_params=pltpu.CompilerParams(
            collective_id=collective_id, has_side_effects=True, vmem_limit_bytes=2 * 1024 * 1024
        ),
        cost_estimate=pl.CostEstimate(
            flops=0, bytes_accessed=4 * devices * rows * columns, transcendentals=0
        ),
        name=name,
    )(shard)


def exchange_kernel(n_ctx, n_dp, widths, input_width, *refs):
    count = len(widths)
    sources, source_input = refs[:count], refs[count]
    targets, target_input = refs[count + 1 : 2 * count + 1], refs[2 * count + 1]
    ctx_send, ctx_recv, dp_send, dp_recv, local_sems = refs[2 * count + 2 :]
    dp = lax.axis_index("dp")
    ctx = lax.axis_index("ctx")
    rows = source_input.shape[0]
    barrier = pltpu.get_barrier_semaphore()
    for turn in range(1, n_ctx):
        pl.semaphore_signal(
            barrier, inc=1, device_id={"ctx": lax.rem(ctx + turn, n_ctx)}, device_id_type=MESH_ID
        )
    for turn in range(1, n_dp):
        pl.semaphore_signal(
            barrier, inc=1, device_id={"dp": lax.rem(dp + turn, n_dp)}, device_id_type=MESH_ID
        )
    pl.semaphore_wait(barrier, n_ctx + n_dp - 2)

    def source(i, peer):
        return sources[i].at[:, pl.ds(pl.multiple_of(peer * widths[i], 128), widths[i])]

    def source_columns(peer):
        return source_input.at[:, pl.ds(pl.multiple_of(peer * input_width, 128), input_width)]

    def row_block(i, owner):
        return targets[i].at[pl.ds(pl.multiple_of(owner * rows, 16), rows)]

    copies = []
    for turn in range(1, n_ctx):
        peer = lax.rem(ctx + turn, n_ctx)
        for i in range(count):
            k = i * (n_ctx - 1) + turn - 1
            copies.append(
                pltpu.make_async_remote_copy(
                    src_ref=source(i, peer),
                    dst_ref=row_block(i, ctx),
                    send_sem=ctx_send.at[k],
                    recv_sem=ctx_recv.at[k],
                    device_id={"ctx": peer},
                    device_id_type=MESH_ID,
                )
            )
            copies[-1].start()
    for turn in range(1, n_dp):
        peer = lax.rem(dp + turn, n_dp)
        copies.append(
            pltpu.make_async_remote_copy(
                src_ref=source_columns(peer),
                dst_ref=target_input.at[dp],
                send_sem=dp_send.at[turn - 1],
                recv_sem=dp_recv.at[turn - 1],
                device_id={"dp": peer},
                device_id_type=MESH_ID,
            )
        )
        copies[-1].start()
    owns = [
        pltpu.make_async_copy(source(i, ctx), row_block(i, ctx), local_sems.at[i])
        for i in range(count)
    ]
    owns.append(
        pltpu.make_async_copy(source_columns(dp), target_input.at[dp], local_sems.at[count])
    )
    for own in owns:
        own.start()
    for own in owns:
        own.wait()
    for turn in range(1, n_ctx):
        origin = lax.rem(ctx + n_ctx - turn, n_ctx)
        for i in range(count):
            k = i * (n_ctx - 1) + turn - 1
            pltpu.make_async_remote_copy(
                src_ref=source(i, origin),
                dst_ref=row_block(i, origin),
                send_sem=ctx_send.at[k],
                recv_sem=ctx_recv.at[k],
                device_id={"ctx": origin},
                device_id_type=MESH_ID,
            ).wait_recv()
    for turn in range(1, n_dp):
        origin = lax.rem(dp + n_dp - turn, n_dp)
        pltpu.make_async_remote_copy(
            src_ref=source_columns(origin),
            dst_ref=target_input.at[origin],
            send_sem=dp_send.at[turn - 1],
            recv_sem=dp_recv.at[turn - 1],
            device_id={"dp": origin},
            device_id_type=MESH_ID,
        ).wait_recv()
    for copy in copies:
        copy.wait_send()


def exchange(arrays, layer_input, n_ctx, n_dp):
    rows = layer_input.shape[0]
    widths = tuple(array.shape[1] // n_ctx for array in arrays)
    input_width = layer_input.shape[1] // n_dp
    dma = pltpu.SemaphoreType.DMA
    ctx_copies = len(arrays) * (n_ctx - 1)
    anywhere = pl.BlockSpec(memory_space=pl.ANY)
    return pl.pallas_call(
        functools.partial(exchange_kernel, n_ctx, n_dp, widths, input_width),
        in_specs=[anywhere] * (len(arrays) + 1),
        out_specs=[anywhere] * (len(arrays) + 1),
        out_shape=[
            jax.ShapeDtypeStruct((rows * n_ctx, width), jnp.bfloat16) for width in widths
        ]
        + [jax.ShapeDtypeStruct((n_dp, rows, input_width), jnp.bfloat16)],
        scratch_shapes=[
            dma((ctx_copies,)),
            dma((ctx_copies,)),
            dma((n_dp - 1,)),
            dma((n_dp - 1,)),
            dma((len(arrays) + 1,)),
        ],
        compiler_params=pltpu.CompilerParams(collective_id=3, has_side_effects=True),
        cost_estimate=pl.CostEstimate(
            flops=0, bytes_accessed=8 * rows * layer_input.shape[1], transcendentals=0
        ),
        name="exchange",
    )(*arrays, layer_input)


def total_kernel(n_ctx, n_dp, x_ref, out_ref, held_dp, part, held_ctx, *sems):
    dp_send, dp_recv, ctx_send, ctx_recv = sems
    dp = lax.axis_index("dp")
    ctx = lax.axis_index("ctx")
    stages = (
        ("dp", dp, n_dp, x_ref, held_dp, dp_send, dp_recv),
        ("ctx", ctx, n_ctx, part, held_ctx, ctx_send, ctx_recv),
    )
    barrier = pltpu.get_barrier_semaphore()
    for axis, me, size, *_ in stages:
        for turn in range(1, size):
            pl.semaphore_signal(
                barrier, inc=1, device_id={axis: lax.rem(me + turn, size)}, device_id_type=MESH_ID
            )
    pl.semaphore_wait(barrier, n_ctx + n_dp - 2)
    for axis, me, size, block, held, send, recv in stages:
        copies = [
            pltpu.make_async_remote_copy(
                src_ref=block,
                dst_ref=held.at[turn - 1],
                send_sem=send.at[turn - 1],
                recv_sem=recv.at[turn - 1],
                device_id={axis: lax.rem(me + turn, size)},
                device_id_type=MESH_ID,
            )
            for turn in range(1, size)
        ]
        for copy in copies:
            copy.start()
        for copy in copies:
            copy.wait()
        total = block[...]
        for turn in range(1, size):
            total += held[turn - 1]
        if axis == "dp":
            part[...] = total
        else:
            out_ref[...] = total


def total_over_devices(first, second, n_ctx, n_dp):
    rows = jnp.arange(8)[:, None]
    block = jnp.where(rows == 0, first, jnp.where(rows == 1, second, 0.0))
    block = jnp.broadcast_to(block, (8, 128)).astype(jnp.float32)
    dma = pltpu.SemaphoreType.DMA
    total = pl.pallas_call(
        functools.partial(total_kernel, n_ctx, n_dp),
        in_specs=[pl.BlockSpec(memory_space=pltpu.VMEM)],
        out_specs=pl.BlockSpec(memory_space=pltpu.VMEM),
        out_shape=jax.ShapeDtypeStruct((8, 128), jnp.float32),
        scratch_shapes=[
            pltpu.VMEM((n_dp - 1, 8, 128), jnp.float32),
            pltpu.VMEM((8, 128), jnp.float32),
            pltpu.VMEM((n_ctx - 1, 8, 128), jnp.float32),
            dma((n_dp - 1,)),
            dma((n_dp - 1,)),
            dma((n_ctx - 1,)),
            dma((n_ctx - 1,)),
        ],
        compiler_params=pltpu.CompilerParams(collective_id=4, has_side_effects=True),
        cost_estimate=pl.CostEstimate(flops=0, bytes_accessed=65536, transcendentals=0),
        name="total",
    )(block)
    return total[0, 0], total[1, 0]


def body(
    devices,
    heads_split,
    layer_input,
    queries,
    keys_saved,
    values_saved,
    out_grad,
    master_weight,
    first_moment,
    second_moment,
):
    weight_sq = jnp.sum(master_weight * master_weight)
    *heads, input_rows = exchange(
        (queries[0], keys_saved[0], values_saved[0], out_grad[0]),
        layer_input[0],
        heads_split,
        devices,
    )
    input_rows = lax.all_gather(input_rows, "ctx", axis=1, tiled=True)
    grouped = head_grads(*heads)
    grouped_all = gather_dp(grouped, devices, 1, "gather_grouped")
    gradient = lax.dot_general(
        input_rows,
        grouped_all,
        (((0, 1), (0, 1)), ((), ())),
        preferred_element_type=jnp.float32,
    )
    first_new = beta_first * first_moment + (1.0 - beta_first) * gradient
    second_new = beta_second * second_moment + (1.0 - beta_second) * gradient * gradient
    corr_first = 1.0 - beta_first**STEP
    corr_second = 1.0 - beta_second**STEP
    direction = (
        first_new / corr_first / (jnp.sqrt(second_new / corr_second) + adam_epsilon)
        + decay_rate * master_weight
    )
    update_sq = jnp.sum(direction * direction)
    weight_total, update_total = total_over_devices(
        weight_sq, update_sq, heads_split, devices
    )
    trust_ratio = jnp.sqrt(weight_total) / jnp.sqrt(update_total)
    lamb_update = trust_ratio * direction
    new_local = (master_weight - learn_rate * lamb_update).astype(jnp.bfloat16)
    new_weights = gather_dp(new_local, devices, 2, "gather_weights")
    return (first_new, second_new, lamb_update, new_weights.reshape(-1, new_local.shape[1]))


def solution(mesh):
    in_specs = (
        P("dp", "ctx", None),
        P("dp", "ctx", None),
        P("dp", "ctx", None),
        P("dp", "ctx", None),
        P("dp", "ctx", None),
        P("dp", "ctx"),
        P("dp", "ctx"),
        P("dp", "ctx"),
    )
    out_specs = (P("dp", "ctx"), P("dp", "ctx"), P("dp", "ctx"), P(None, "ctx"))
    return jax.shard_map(
        functools.partial(body, mesh.shape["dp"], mesh.shape["ctx"]),
        mesh=mesh,
        in_specs=in_specs,
        out_specs=out_specs,
        check_vma=False,
    )
```

```python
import functools

import jax
import jax.numpy as jnp
from jax import lax
from jax.experimental import pallas as pl
from jax.experimental.pallas import tpu as pltpu
from jax.sharding import PartitionSpec as P

HEAD_DIM = 128
STEP = 100


beta_first = 0.9
beta_second = 0.999
adam_epsilon = 1e-06
decay_rate = 0.01
learn_rate = 0.01
masked_score = -1e30

MESH_ID = pl.DeviceIdType.MESH
SLOW = 4


def nt(left, right):
    return lax.dot_general(
        left, right, (((1,), (1,)), ((), ())), preferred_element_type=jnp.float32
    )


def nn(left, right):
    return jnp.dot(left, right, preferred_element_type=jnp.float32)


def head_grads(group, block, kv, q_ref, k_ref, v_ref, g_ref, out_ref, dk_acc, dv_acc):
    length = q_ref.shape[0]
    scale = HEAD_DIM ** (-0.5)
    width = group * HEAD_DIM
    base = kv * (width + 2 * HEAD_DIM)
    kv_columns = slice(kv * HEAD_DIM, (kv + 1) * HEAD_DIM)
    dk_acc[...] = jnp.zeros_like(dk_acc)
    dv_acc[...] = jnp.zeros_like(dv_acc)

    def one_head(head, carry):
        here = pl.ds(pl.multiple_of(kv * width + head * HEAD_DIM, HEAD_DIM), HEAD_DIM)
        there = pl.ds(pl.multiple_of(base + head * HEAD_DIM, HEAD_DIM), HEAD_DIM)
        for start in range(0, length, block):
            keys = start + block
            query = q_ref[start:keys, here]
            grad = g_ref[start:keys, here]
            key = k_ref[:keys, kv_columns]
            value = v_ref[:keys, kv_columns]
            scores = nt(key, query) * scale
            row = lax.broadcasted_iota(jnp.int32, (keys, block), 0)
            column = lax.broadcasted_iota(jnp.int32, (keys, block), 1) + start
            scores = jnp.where(row <= column, scores, masked_score)
            weights = jnp.exp(scores - jnp.max(scores, axis=0, keepdims=True))
            probs = weights / jnp.sum(weights, axis=0, keepdims=True)
            probs_b = probs.astype(jnp.bfloat16)
            prob_grad = nt(value, grad)
            row_delta = jnp.sum(probs_b.astype(jnp.float32) * prob_grad, axis=0, keepdims=True)
            dscore = (probs * (prob_grad - row_delta)).astype(jnp.bfloat16)
            dq = lax.dot_general(
                dscore, key, (((0,), (0,)), ((), ())), preferred_element_type=jnp.float32
            )
            out_ref[start:keys, there] = (dq * scale).astype(jnp.bfloat16)
            dk_acc[:keys, :] += nn(dscore, query)
            dv_acc[:keys, :] += nn(probs_b, grad)
        return carry

    lax.fori_loop(0, group, one_head, 0)
    split = base + width
    out_ref[:, split : split + HEAD_DIM] = (dk_acc[...] * scale).astype(jnp.bfloat16)
    out_ref[:, split + HEAD_DIM : split + 2 * HEAD_DIM] = dv_acc[...].astype(jnp.bfloat16)


def gather_kernel(slow, fast, chunks, tail, x_ref, out_ref, *sems, enter=None, produce=None, relay=None):
    local_sem, p1s, p1r, x1s, x1r, x2s, x2r, p2s, p2r = sems
    me = lax.axis_index("dp")
    a = me // fast
    b = lax.rem(me, fast)
    lines = {"a": (a, slow, fast), "b": (b, fast, 1)}
    n_chunks = len(chunks)

    def neighbour(line, way):
        return me + way * lines[line][2]

    def can(line, way):
        pos, size, _ = lines[line]
        return pos + 1 < size if way > 0 else pos > 0

    if enter is None:
        barrier = pltpu.get_barrier_semaphore()
        for line in ("a", "b"):
            for way in (1, -1):

                @pl.when(can(line, way))
                def _(line=line, way=way):
                    pl.semaphore_signal(
                        barrier,
                        inc=1,
                        device_id={"dp": neighbour(line, way)},
                        device_id_type=MESH_ID,
                    )

        neighbours = sum(
            can(line, way).astype(jnp.int32) for line in ("a", "b") for way in (1, -1)
        )
        pl.semaphore_wait(barrier, neighbours)
    else:
        enter()

    local = pltpu.make_async_copy(x_ref, out_ref.at[me], local_sem)

    def piece(origin, rows, own):
        part = (pl.ds(*rows[:2]), pl.ds(*rows[2:]))
        if own:
            return x_ref.at[part]
        return out_ref.at[(origin, *part)]

    def copy(line, way, origin, rows, own, send, recv):
        return pltpu.make_async_remote_copy(
            src_ref=piece(origin, rows, own),
            dst_ref=piece(origin, rows, False),
            send_sem=send,
            recv_sem=recv,
            device_id={"dp": neighbour(line, way)},
            device_id_type=MESH_ID,
        )

    pending = []

    def send(condition, *args):
        @pl.when(condition)
        def _():
            copy(*args).start()

        pending.append((condition, args))

    def both(first, second):
        return jnp.logical_and(first, second)

    def send_a1(step, c, way):
        origin_a = a - way * step
        inside = origin_a >= 0 if way > 0 else origin_a < slow
        d = 0 if way > 0 else 1
        i = (d * (slow - 1) + step) * n_chunks + c
        send(
            both(can("a", way), inside),
            "a", way, origin_a * fast + b, chunks[c], step == 0, p1s.at[i], p1r.at[i],
        )

    def recv_a1(step, c, way):
        origin_a = a - way * (step + 1)
        inside = origin_a >= 0 if way > 0 else origin_a < slow
        d = 0 if way > 0 else 1
        i = (d * (slow - 1) + step) * n_chunks + c

        @pl.when(inside)
        def _():
            copy("a", -way, origin_a * fast + b, chunks[c], False, p1s.at[i], p1r.at[i]).wait_recv()

        return inside, origin_a

    def send_b1(step, slot, c, way, present):
        origin_a = a + slot
        origin_b = b - way * step
        inside = origin_b >= 0 if way > 0 else origin_b < fast
        d = 0 if way > 0 else 1
        i = ((d * (fast - 1) + step) * (2 * slow - 1) + slot + slow - 1) * n_chunks + c
        send(
            both(present, both(can("b", way), inside)),
            "b", way, origin_a * fast + origin_b, chunks[c], step == 0 and slot == 0,
            x1s.at[i], x1r.at[i],
        )

    def recv_b1(step, slot, c, way):
        origin_a = a + slot
        present = both(origin_a >= 0, origin_a < slow)
        origin_b = b - way * (step + 1)
        inside = origin_b >= 0 if way > 0 else origin_b < fast
        d = 0 if way > 0 else 1
        i = ((d * (fast - 1) + step) * (2 * slow - 1) + slot + slow - 1) * n_chunks + c

        @pl.when(both(present, inside))
        def _():
            copy(
                "b", -way, origin_a * fast + origin_b, chunks[c], False, x1s.at[i], x1r.at[i]
            ).wait_recv()

        return present

    def send_b2(step, way):
        origin_b = b - way * step
        inside = origin_b >= 0 if way > 0 else origin_b < fast
        i = (0 if way > 0 else 1) * (fast - 1) + step
        send(
            both(can("b", way), inside),
            "b", way, a * fast + origin_b, tail, step == 0, x2s.at[i], x2r.at[i],
        )

    def recv_b2(step, way):
        origin_b = b - way * (step + 1)
        inside = origin_b >= 0 if way > 0 else origin_b < fast
        i = (0 if way > 0 else 1) * (fast - 1) + step

        @pl.when(inside)
        def _():
            copy("b", -way, a * fast + origin_b, tail, False, x2s.at[i], x2r.at[i]).wait_recv()

        return inside

    def send_a2(step, turn, way):
        origin_a = a - way * step
        inside = origin_a >= 0 if way > 0 else origin_a < slow
        origin_b = lax.rem(b + turn, fast)
        i = ((0 if way > 0 else 1) * (slow - 1) + step) * fast + turn
        send(
            both(can("a", way), inside),
            "a", way, origin_a * fast + origin_b, tail, step == 0 and turn == 0,
            p2s.at[i], p2r.at[i],
        )

    def recv_a2(step, turn, way):
        origin_a = a - way * (step + 1)
        inside = origin_a >= 0 if way > 0 else origin_a < slow
        origin_b = lax.rem(b + turn, fast)
        i = ((0 if way > 0 else 1) * (slow - 1) + step) * fast + turn

        @pl.when(inside)
        def _():
            copy(
                "a", -way, origin_a * fast + origin_b, tail, False, p2s.at[i], p2r.at[i]
            ).wait_recv()

    ways = (1, -1)
    always = a >= 0
    for c in range(n_chunks):
        if produce is not None:
            produce(chunks[c][2] + chunks[c][3])
        for way in ways:
            send_a1(0, c, way)
        for way in ways:
            send_b1(0, 0, c, way, always)
    local.start()
    for way in ways:
        send_b2(0, way)
    if relay is not None:
        relay()
    for step in range(slow - 1):
        for c in range(n_chunks):
            for way in ways:
                present, _ = recv_a1(step, c, way)
                if step + 1 < slow - 1:
                    send_a1(step + 1, c, way)
                for way_b in ways:
                    send_b1(0, -way * (step + 1), c, way_b, present)
    for way in ways:
        send_a2(0, 0, way)
    for hop in range(fast - 1):
        for way in ways:
            recv_b2(hop, way)
            if hop + 1 < fast - 1:
                send_b2(hop + 1, way)
    for turn in range(1, fast):
        for way in ways:
            send_a2(0, turn, way)
    for step in range(slow - 1):
        for turn in range(fast):
            for way in ways:
                recv_a2(step, turn, way)
                if step + 1 < slow - 1:
                    send_a2(step + 1, turn, way)
    slots = [0] + [sign * far for far in range(1, slow) for sign in (-1, 1)]
    for hop in range(fast - 1):
        for slot in slots:
            for c in range(n_chunks):
                for way in ways:
                    present = recv_b1(hop, slot, c, way)
                    if hop + 1 < fast - 1:
                        send_b1(hop + 1, slot, c, way, present)
    local.wait()
    for condition, args in pending:

        @pl.when(condition)
        def _(args=args):
            copy(*args).wait_send()


def gather_plan(rows, columns, devices):
    slow = SLOW
    fast = devices // SLOW
    first = rows * 13 // 16 // 32 * 32
    half = first // 32 * 16
    wide = columns // 2
    chunks = tuple(
        (start, size, column, wide)
        for column in (0, wide)
        for start, size in ((0, half), (half, first - half))
    )
    tail = (first, rows - first, 0, columns)
    n_chunks = len(chunks)
    dma = pltpu.SemaphoreType.DMA
    sizes = (
        2 * (slow - 1) * n_chunks,
        2 * (fast - 1) * (2 * slow - 1) * n_chunks,
        2 * (fast - 1),
        2 * (slow - 1) * fast,
    )
    semaphores = [dma] + [dma((size,)) for size in sizes for _ in range(2)]
    return (slow, fast, chunks, tail), semaphores


def gather_dp(shard, devices, collective_id, name):
    rows, columns = shard.shape
    shape, semaphores = gather_plan(rows, columns, devices)
    return pl.pallas_call(
        functools.partial(gather_kernel, *shape),
        in_specs=[pl.BlockSpec(memory_space=pl.ANY)],
        out_specs=pl.BlockSpec(memory_space=pl.ANY),
        out_shape=jax.ShapeDtypeStruct((devices, rows, columns), shard.dtype),
        scratch_shapes=semaphores,
        compiler_params=pltpu.CompilerParams(
            collective_id=collective_id, has_side_effects=True, vmem_limit_bytes=2 * 1024 * 1024
        ),
        cost_estimate=pl.CostEstimate(
            flops=0, bytes_accessed=4 * devices * rows * columns, transcendentals=0
        ),
        name=name,
    )(shard)


def front_kernel(n_ctx, n_dp, widths, input_width, shape, *refs):
    count = len(widths)
    sources, source_input = refs[:count], refs[count]
    out_ref, target_input = refs[count + 1 : count + 3]
    targets = refs[count + 3 : 2 * count + 3]
    rest = refs[2 * count + 3 :]
    grouped, dk_acc, dv_acc, ctx_send, ctx_recv, dp_send, dp_recv, token_send, token_recv = rest[:9]
    local_sems = rest[9]
    dp = lax.axis_index("dp")
    ctx = lax.axis_index("ctx")
    rows = source_input.shape[0]
    kv_local = widths[1] // HEAD_DIM
    group = widths[0] // widths[1]
    steps = tuple(width // kv_local for width in widths)
    remote = []

    def source(i, kv, peer):
        start = pl.multiple_of(peer * widths[i] + kv * steps[i], 128)
        return sources[i].at[:, pl.ds(start, steps[i])]

    def target(i, kv, owner):
        start = pl.multiple_of(owner * rows, 16)
        return targets[i].at[pl.ds(start, rows), pl.ds(kv * steps[i], steps[i])]

    def source_columns(peer):
        return source_input.at[:, pl.ds(pl.multiple_of(peer * input_width, 128), input_width)]

    def input_block(owner):
        return target_input.at[owner, pl.ds(pl.multiple_of(ctx * rows, 16), rows)]

    def input_tokens(owner):
        return target_input.at[:, pl.ds(pl.multiple_of(owner * rows, 16), rows)]

    def token_copy(turn, peer, owner):
        return pltpu.make_async_remote_copy(
            src_ref=input_tokens(owner),
            dst_ref=input_tokens(owner),
            send_sem=token_send.at[turn - 1],
            recv_sem=token_recv.at[turn - 1],
            device_id={"ctx": peer},
            device_id_type=MESH_ID,
        )

    def ctx_copy(i, kv, turn, peer, owner):
        k = (kv * count + i) * (n_ctx - 1) + turn - 1
        return pltpu.make_async_remote_copy(
            src_ref=source(i, kv, peer),
            dst_ref=target(i, kv, owner),
            send_sem=ctx_send.at[k],
            recv_sem=ctx_recv.at[k],
            device_id={"ctx": peer},
            device_id_type=MESH_ID,
        )

    def input_copy(turn, peer, owner):
        return pltpu.make_async_remote_copy(
            src_ref=source_columns(peer),
            dst_ref=input_block(owner),
            send_sem=dp_send.at[turn - 1],
            recv_sem=dp_recv.at[turn - 1],
            device_id={"dp": peer},
            device_id_type=MESH_ID,
        )

    def own(i, kv):
        return pltpu.make_async_copy(
            source(i, kv, ctx), target(i, kv, ctx), local_sems.at[kv * count + i]
        )

    own_input = pltpu.make_async_copy(
        source_columns(dp), input_block(dp), local_sems.at[kv_local * count]
    )

    def enter():
        barrier = pltpu.get_barrier_semaphore()
        for axis, me, size in (("ctx", ctx, n_ctx), ("dp", dp, n_dp)):
            for turn in range(1, size):
                pl.semaphore_signal(
                    barrier,
                    inc=1,
                    device_id={axis: lax.rem(me + turn, size)},
                    device_id_type=MESH_ID,
                )
        pl.semaphore_wait(barrier, n_ctx + n_dp - 2)
        for kv in range(kv_local):
            for i in range(count):
                for turn in range(1, n_ctx):
                    copy = ctx_copy(i, kv, turn, lax.rem(ctx + turn, n_ctx), ctx)
                    copy.start()
                    remote.append(copy)
                own(i, kv).start()
        for turn in range(1, n_dp):
            copy = input_copy(turn, lax.rem(dp + turn, n_dp), dp)
            copy.start()
            remote.append(copy)
        own_input.start()

    made = []

    def produce(column):
        while len(made) * (group + 2) * HEAD_DIM < column:
            kv = len(made)
            for i in range(count):
                own(i, kv).wait()
                for turn in range(1, n_ctx):
                    origin = lax.rem(ctx + n_ctx - turn, n_ctx)
                    ctx_copy(i, kv, turn, origin, origin).wait_recv()
            block = min(256, rows * n_ctx)
            head_grads(group, block, kv, *targets, grouped, dk_acc, dv_acc)
            made.append(kv)

    def relay():
        own_input.wait()
        for turn in range(1, n_dp):
            origin = lax.rem(dp + n_dp - turn, n_dp)
            input_copy(turn, origin, origin).wait_recv()
        for turn in range(1, n_ctx):
            copy = token_copy(turn, lax.rem(ctx + turn, n_ctx), ctx)
            copy.start()
            remote.append(copy)

    gather_kernel(
        *shape, grouped, out_ref, *rest[10:], enter=enter, produce=produce, relay=relay
    )
    for turn in range(1, n_ctx):
        origin = lax.rem(ctx + n_ctx - turn, n_ctx)
        token_copy(turn, origin, origin).wait_recv()
    for copy in remote:
        copy.wait_send()


def front(arrays, layer_input, n_ctx, n_dp):
    rows = layer_input.shape[0]
    length = rows * n_ctx
    widths = tuple(array.shape[1] // n_ctx for array in arrays)
    input_width = layer_input.shape[1] // n_dp
    columns = widths[0] + 2 * widths[1]
    kv_local = widths[1] // HEAD_DIM
    shape, semaphores = gather_plan(length, columns, n_dp)
    dma = pltpu.SemaphoreType.DMA
    ctx_copies = len(arrays) * (n_ctx - 1) * kv_local
    anywhere = pl.BlockSpec(memory_space=pl.ANY)
    return pl.pallas_call(
        functools.partial(front_kernel, n_ctx, n_dp, widths, input_width, shape),
        in_specs=[anywhere] * (len(arrays) + 1),
        out_specs=[anywhere] * 2,
        out_shape=[
            jax.ShapeDtypeStruct((n_dp, length, columns), jnp.bfloat16),
            jax.ShapeDtypeStruct((n_dp, length, input_width), jnp.bfloat16),
        ],
        scratch_shapes=[pltpu.VMEM((length, width), jnp.bfloat16) for width in widths]
        + [
            pltpu.VMEM((length, columns), jnp.bfloat16),
            pltpu.VMEM((length, HEAD_DIM), jnp.float32),
            pltpu.VMEM((length, HEAD_DIM), jnp.float32),
            dma((ctx_copies,)),
            dma((ctx_copies,)),
            dma((n_dp - 1,)),
            dma((n_dp - 1,)),
            dma((n_ctx - 1,)),
            dma((n_ctx - 1,)),
            dma((len(arrays) * kv_local + 1,)),
        ]
        + semaphores,
        compiler_params=pltpu.CompilerParams(
            collective_id=3, has_side_effects=True, vmem_limit_bytes=28 * 1024 * 1024
        ),
        cost_estimate=pl.CostEstimate(
            flops=10 * length * length * widths[0],
            bytes_accessed=4 * n_dp * length * columns,
            transcendentals=length * length * widths[0] // HEAD_DIM,
        ),
        name="front",
    )(*arrays, layer_input)


def total_kernel(n_ctx, n_dp, x_ref, out_ref, held_dp, part, held_ctx, *sems):
    dp_send, dp_recv, ctx_send, ctx_recv = sems
    dp = lax.axis_index("dp")
    ctx = lax.axis_index("ctx")
    stages = (
        ("dp", dp, n_dp, x_ref, held_dp, dp_send, dp_recv),
        ("ctx", ctx, n_ctx, part, held_ctx, ctx_send, ctx_recv),
    )
    barrier = pltpu.get_barrier_semaphore()
    for axis, me, size, *_ in stages:
        for turn in range(1, size):
            pl.semaphore_signal(
                barrier, inc=1, device_id={axis: lax.rem(me + turn, size)}, device_id_type=MESH_ID
            )
    pl.semaphore_wait(barrier, n_ctx + n_dp - 2)
    for axis, me, size, block, held, send, recv in stages:
        copies = [
            pltpu.make_async_remote_copy(
                src_ref=block,
                dst_ref=held.at[turn - 1],
                send_sem=send.at[turn - 1],
                recv_sem=recv.at[turn - 1],
                device_id={axis: lax.rem(me + turn, size)},
                device_id_type=MESH_ID,
            )
            for turn in range(1, size)
        ]
        for copy in copies:
            copy.start()
        for copy in copies:
            copy.wait()
        total = block[...]
        for turn in range(1, size):
            total += held[turn - 1]
        if axis == "dp":
            part[...] = total
        else:
            out_ref[...] = total


def total_over_devices(first, second, n_ctx, n_dp):
    rows = jnp.arange(8)[:, None]
    block = jnp.where(rows == 0, first, jnp.where(rows == 1, second, 0.0))
    block = jnp.broadcast_to(block, (8, 128)).astype(jnp.float32)
    dma = pltpu.SemaphoreType.DMA
    total = pl.pallas_call(
        functools.partial(total_kernel, n_ctx, n_dp),
        in_specs=[pl.BlockSpec(memory_space=pltpu.VMEM)],
        out_specs=pl.BlockSpec(memory_space=pltpu.VMEM),
        out_shape=jax.ShapeDtypeStruct((8, 128), jnp.float32),
        scratch_shapes=[
            pltpu.VMEM((n_dp - 1, 8, 128), jnp.float32),
            pltpu.VMEM((8, 128), jnp.float32),
            pltpu.VMEM((n_ctx - 1, 8, 128), jnp.float32),
            dma((n_dp - 1,)),
            dma((n_dp - 1,)),
            dma((n_ctx - 1,)),
            dma((n_ctx - 1,)),
        ],
        compiler_params=pltpu.CompilerParams(collective_id=4, has_side_effects=True),
        cost_estimate=pl.CostEstimate(flops=0, bytes_accessed=65536, transcendentals=0),
        name="total",
    )(block)
    return total[0, 0], total[1, 0]


def body(
    devices,
    heads_split,
    layer_input,
    queries,
    keys_saved,
    values_saved,
    out_grad,
    master_weight,
    first_moment,
    second_moment,
):
    weight_sq = jnp.sum(master_weight * master_weight)
    grouped_all, input_rows = front(
        (queries[0], keys_saved[0], values_saved[0], out_grad[0]),
        layer_input[0],
        heads_split,
        devices,
    )
    gradient = lax.dot_general(
        input_rows,
        grouped_all,
        (((0, 1), (0, 1)), ((), ())),
        preferred_element_type=jnp.float32,
    )
    first_new = beta_first * first_moment + (1.0 - beta_first) * gradient
    second_new = beta_second * second_moment + (1.0 - beta_second) * gradient * gradient
    corr_first = 1.0 - beta_first**STEP
    corr_second = 1.0 - beta_second**STEP
    direction = (
        first_new / corr_first / (jnp.sqrt(second_new / corr_second) + adam_epsilon)
        + decay_rate * master_weight
    )
    update_sq = jnp.sum(direction * direction)
    weight_total, update_total = total_over_devices(
        weight_sq, update_sq, heads_split, devices
    )
    trust_ratio = jnp.sqrt(weight_total) / jnp.sqrt(update_total)
    lamb_update = trust_ratio * direction
    new_local = (master_weight - learn_rate * lamb_update).astype(jnp.bfloat16)
    new_weights = gather_dp(new_local, devices, 2, "gather_weights")
    return (first_new, second_new, lamb_update, new_weights.reshape(-1, new_local.shape[1]))


def solution(mesh):
    in_specs = (
        P("dp", "ctx", None),
        P("dp", "ctx", None),
        P("dp", "ctx", None),
        P("dp", "ctx", None),
        P("dp", "ctx", None),
        P("dp", "ctx"),
        P("dp", "ctx"),
        P("dp", "ctx"),
    )
    out_specs = (P("dp", "ctx"), P("dp", "ctx"), P("dp", "ctx"), P(None, "ctx"))
    return jax.shard_map(
        functools.partial(body, mesh.shape["dp"], mesh.shape["ctx"]),
        mesh=mesh,
        in_specs=in_specs,
        out_specs=out_specs,
        check_vma=False,
    )
```

```python
import functools

import jax
import jax.numpy as jnp
from jax import lax
from jax.experimental import pallas as pl
from jax.experimental.pallas import tpu as pltpu
from jax.sharding import PartitionSpec as P

HEAD_DIM = 128
STEP = 100


beta_first = 0.9
beta_second = 0.999
adam_epsilon = 1e-06
decay_rate = 0.01
learn_rate = 0.01
masked_score = -1e30

MESH_ID = pl.DeviceIdType.MESH
SLOW = 4


def nt(left, right):
    return lax.dot_general(
        left, right, (((1,), (1,)), ((), ())), preferred_element_type=jnp.float32
    )


def nn(left, right):
    return jnp.dot(left, right, preferred_element_type=jnp.float32)


def head_grads(group, block, kv, q_ref, k_ref, v_ref, g_ref, out_ref, dk_acc, dv_acc):
    length = q_ref.shape[0]
    scale = HEAD_DIM ** (-0.5)
    width = group * HEAD_DIM
    base = kv * (width + 2 * HEAD_DIM)
    kv_columns = slice(kv * HEAD_DIM, (kv + 1) * HEAD_DIM)
    dk_acc[...] = jnp.zeros_like(dk_acc)
    dv_acc[...] = jnp.zeros_like(dv_acc)

    def one_head(head, carry):
        here = pl.ds(pl.multiple_of(kv * width + head * HEAD_DIM, HEAD_DIM), HEAD_DIM)
        there = pl.ds(pl.multiple_of(base + head * HEAD_DIM, HEAD_DIM), HEAD_DIM)
        for start in range(0, length, block):
            keys = start + block
            query = q_ref[start:keys, here]
            grad = g_ref[start:keys, here]
            key = k_ref[:keys, kv_columns]
            value = v_ref[:keys, kv_columns]
            scores = nt(key, query) * scale
            row = lax.broadcasted_iota(jnp.int32, (keys, block), 0)
            column = lax.broadcasted_iota(jnp.int32, (keys, block), 1) + start
            scores = jnp.where(row <= column, scores, masked_score)
            weights = jnp.exp(scores - jnp.max(scores, axis=0, keepdims=True))
            probs = weights / jnp.sum(weights, axis=0, keepdims=True)
            probs_b = probs.astype(jnp.bfloat16)
            prob_grad = nt(value, grad)
            row_delta = jnp.sum(probs_b.astype(jnp.float32) * prob_grad, axis=0, keepdims=True)
            dscore = (probs * (prob_grad - row_delta)).astype(jnp.bfloat16)
            dq = lax.dot_general(
                dscore, key, (((0,), (0,)), ((), ())), preferred_element_type=jnp.float32
            )
            out_ref[start:keys, there] = (dq * scale).astype(jnp.bfloat16)
            dk_acc[:keys, :] += nn(dscore, query)
            dv_acc[:keys, :] += nn(probs_b, grad)
        return carry

    lax.fori_loop(0, group, one_head, 0)
    split = base + width
    out_ref[:, split : split + HEAD_DIM] = (dk_acc[...] * scale).astype(jnp.bfloat16)
    out_ref[:, split + HEAD_DIM : split + 2 * HEAD_DIM] = dv_acc[...].astype(jnp.bfloat16)


def gather_kernel(slow, fast, chunks, tail, x_ref, out_ref, *sems, enter=None, produce=None, relay=None):
    local_sem, p1s, p1r, x1s, x1r, x2s, x2r, p2s, p2r = sems
    me = lax.axis_index("dp")
    a = me // fast
    b = lax.rem(me, fast)
    lines = {"a": (a, slow, fast), "b": (b, fast, 1)}
    n_chunks = len(chunks)

    def neighbour(line, way):
        return me + way * lines[line][2]

    def can(line, way):
        pos, size, _ = lines[line]
        return pos + 1 < size if way > 0 else pos > 0

    if enter is None:
        barrier = pltpu.get_barrier_semaphore()
        for line in ("a", "b"):
            for way in (1, -1):

                @pl.when(can(line, way))
                def _(line=line, way=way):
                    pl.semaphore_signal(
                        barrier,
                        inc=1,
                        device_id={"dp": neighbour(line, way)},
                        device_id_type=MESH_ID,
                    )

        neighbours = sum(
            can(line, way).astype(jnp.int32) for line in ("a", "b") for way in (1, -1)
        )
        pl.semaphore_wait(barrier, neighbours)
    else:
        enter()

    local = pltpu.make_async_copy(x_ref, out_ref.at[me], local_sem)

    def piece(origin, rows, own):
        part = (pl.ds(*rows[:2]), pl.ds(*rows[2:]))
        if own:
            return x_ref.at[part]
        return out_ref.at[(origin, *part)]

    def copy(line, way, origin, rows, own, send, recv):
        return pltpu.make_async_remote_copy(
            src_ref=piece(origin, rows, own),
            dst_ref=piece(origin, rows, False),
            send_sem=send,
            recv_sem=recv,
            device_id={"dp": neighbour(line, way)},
            device_id_type=MESH_ID,
        )

    pending = []

    def send(condition, *args):
        @pl.when(condition)
        def _():
            copy(*args).start()

        pending.append((condition, args))

    def both(first, second):
        return jnp.logical_and(first, second)

    def send_a1(step, c, way):
        origin_a = a - way * step
        inside = origin_a >= 0 if way > 0 else origin_a < slow
        d = 0 if way > 0 else 1
        i = (d * (slow - 1) + step) * n_chunks + c
        send(
            both(can("a", way), inside),
            "a", way, origin_a * fast + b, chunks[c], step == 0, p1s.at[i], p1r.at[i],
        )

    def recv_a1(step, c, way):
        origin_a = a - way * (step + 1)
        inside = origin_a >= 0 if way > 0 else origin_a < slow
        d = 0 if way > 0 else 1
        i = (d * (slow - 1) + step) * n_chunks + c

        @pl.when(inside)
        def _():
            copy("a", -way, origin_a * fast + b, chunks[c], False, p1s.at[i], p1r.at[i]).wait_recv()

        return inside, origin_a

    def send_b1(step, slot, c, way, present):
        origin_a = a + slot
        origin_b = b - way * step
        inside = origin_b >= 0 if way > 0 else origin_b < fast
        d = 0 if way > 0 else 1
        i = ((d * (fast - 1) + step) * (2 * slow - 1) + slot + slow - 1) * n_chunks + c
        send(
            both(present, both(can("b", way), inside)),
            "b", way, origin_a * fast + origin_b, chunks[c], step == 0 and slot == 0,
            x1s.at[i], x1r.at[i],
        )

    def recv_b1(step, slot, c, way):
        origin_a = a + slot
        present = both(origin_a >= 0, origin_a < slow)
        origin_b = b - way * (step + 1)
        inside = origin_b >= 0 if way > 0 else origin_b < fast
        d = 0 if way > 0 else 1
        i = ((d * (fast - 1) + step) * (2 * slow - 1) + slot + slow - 1) * n_chunks + c

        @pl.when(both(present, inside))
        def _():
            copy(
                "b", -way, origin_a * fast + origin_b, chunks[c], False, x1s.at[i], x1r.at[i]
            ).wait_recv()

        return present

    def send_b2(step, way):
        origin_b = b - way * step
        inside = origin_b >= 0 if way > 0 else origin_b < fast
        i = (0 if way > 0 else 1) * (fast - 1) + step
        send(
            both(can("b", way), inside),
            "b", way, a * fast + origin_b, tail, step == 0, x2s.at[i], x2r.at[i],
        )

    def recv_b2(step, way):
        origin_b = b - way * (step + 1)
        inside = origin_b >= 0 if way > 0 else origin_b < fast
        i = (0 if way > 0 else 1) * (fast - 1) + step

        @pl.when(inside)
        def _():
            copy("b", -way, a * fast + origin_b, tail, False, x2s.at[i], x2r.at[i]).wait_recv()

        return inside

    def send_a2(step, turn, way):
        origin_a = a - way * step
        inside = origin_a >= 0 if way > 0 else origin_a < slow
        origin_b = lax.rem(b + turn, fast)
        i = ((0 if way > 0 else 1) * (slow - 1) + step) * fast + turn
        send(
            both(can("a", way), inside),
            "a", way, origin_a * fast + origin_b, tail, step == 0 and turn == 0,
            p2s.at[i], p2r.at[i],
        )

    def recv_a2(step, turn, way):
        origin_a = a - way * (step + 1)
        inside = origin_a >= 0 if way > 0 else origin_a < slow
        origin_b = lax.rem(b + turn, fast)
        i = ((0 if way > 0 else 1) * (slow - 1) + step) * fast + turn

        @pl.when(inside)
        def _():
            copy(
                "a", -way, origin_a * fast + origin_b, tail, False, p2s.at[i], p2r.at[i]
            ).wait_recv()

    ways = (1, -1)
    always = a >= 0
    for c in range(n_chunks):
        if produce is not None:
            produce(chunks[c][2] + chunks[c][3])
        for way in ways:
            send_a1(0, c, way)
        for way in ways:
            send_b1(0, 0, c, way, always)
    local.start()
    for way in ways:
        send_b2(0, way)
    if relay is not None:
        relay()
    for step in range(slow - 1):
        for c in range(n_chunks):
            for way in ways:
                present, _ = recv_a1(step, c, way)
                if step + 1 < slow - 1:
                    send_a1(step + 1, c, way)
                for way_b in ways:
                    send_b1(0, -way * (step + 1), c, way_b, present)
    for way in ways:
        send_a2(0, 0, way)
    for hop in range(fast - 1):
        for way in ways:
            recv_b2(hop, way)
            if hop + 1 < fast - 1:
                send_b2(hop + 1, way)
    for turn in range(1, fast):
        for way in ways:
            send_a2(0, turn, way)
    for step in range(slow - 1):
        for turn in range(fast):
            for way in ways:
                recv_a2(step, turn, way)
                if step + 1 < slow - 1:
                    send_a2(step + 1, turn, way)
    slots = [0] + [sign * far for far in range(1, slow) for sign in (-1, 1)]
    for hop in range(fast - 1):
        for slot in slots:
            for c in range(n_chunks):
                for way in ways:
                    present = recv_b1(hop, slot, c, way)
                    if hop + 1 < fast - 1:
                        send_b1(hop + 1, slot, c, way, present)
    local.wait()
    for condition, args in pending:

        @pl.when(condition)
        def _(args=args):
            copy(*args).wait_send()


def gather_plan(rows, columns, devices):
    slow = SLOW
    fast = devices // SLOW
    first = rows * 13 // 16 // 32 * 32
    half = first // 32 * 16
    wide = columns // 2
    chunks = tuple(
        (start, size, column, wide)
        for column in (0, wide)
        for start, size in ((0, half), (half, first - half))
    )
    tail = (first, rows - first, 0, columns)
    n_chunks = len(chunks)
    dma = pltpu.SemaphoreType.DMA
    sizes = (
        2 * (slow - 1) * n_chunks,
        2 * (fast - 1) * (2 * slow - 1) * n_chunks,
        2 * (fast - 1),
        2 * (slow - 1) * fast,
    )
    semaphores = [dma] + [dma((size,)) for size in sizes for _ in range(2)]
    return (slow, fast, chunks, tail), semaphores


def gather_dp(shard, devices, collective_id, name):
    rows, columns = shard.shape
    shape, semaphores = gather_plan(rows, columns, devices)
    return pl.pallas_call(
        functools.partial(gather_kernel, *shape),
        in_specs=[pl.BlockSpec(memory_space=pl.ANY)],
        out_specs=pl.BlockSpec(memory_space=pl.ANY),
        out_shape=jax.ShapeDtypeStruct((devices, rows, columns), shard.dtype),
        scratch_shapes=semaphores,
        compiler_params=pltpu.CompilerParams(
            collective_id=collective_id, has_side_effects=True, vmem_limit_bytes=2 * 1024 * 1024
        ),
        cost_estimate=pl.CostEstimate(
            flops=0, bytes_accessed=4 * devices * rows * columns, transcendentals=0
        ),
        name=name,
    )(shard)


def front_kernel(n_ctx, n_dp, widths, input_width, shape, *refs):
    count = len(widths)
    sources, source_input = refs[:count], refs[count]
    out_ref, target_input = refs[count + 1 : count + 3]
    targets = refs[count + 3 : 2 * count + 3]
    rest = refs[2 * count + 3 :]
    grouped, dk_acc, dv_acc, ctx_send, ctx_recv, dp_send, dp_recv, token_send, token_recv = rest[:9]
    local_sems = rest[9]
    dp = lax.axis_index("dp")
    ctx = lax.axis_index("ctx")
    rows = source_input.shape[0]
    kv_local = widths[1] // HEAD_DIM
    group = widths[0] // widths[1]
    steps = tuple(width // kv_local for width in widths)
    remote = []

    def source(i, kv, peer):
        start = pl.multiple_of(peer * widths[i] + kv * steps[i], 128)
        return sources[i].at[:, pl.ds(start, steps[i])]

    def target(i, kv, owner):
        start = pl.multiple_of(owner * rows, 16)
        return targets[i].at[pl.ds(start, rows), pl.ds(kv * steps[i], steps[i])]

    def source_columns(peer):
        return source_input.at[:, pl.ds(pl.multiple_of(peer * input_width, 128), input_width)]

    def input_block(owner):
        return target_input.at[owner, pl.ds(pl.multiple_of(ctx * rows, 16), rows)]

    def input_tokens(owner):
        return target_input.at[:, pl.ds(pl.multiple_of(owner * rows, 16), rows)]

    def token_copy(turn, peer, owner):
        return pltpu.make_async_remote_copy(
            src_ref=input_tokens(owner),
            dst_ref=input_tokens(owner),
            send_sem=token_send.at[turn - 1],
            recv_sem=token_recv.at[turn - 1],
            device_id={"ctx": peer},
            device_id_type=MESH_ID,
        )

    def ctx_copy(i, kv, turn, peer, owner):
        k = (kv * count + i) * (n_ctx - 1) + turn - 1
        return pltpu.make_async_remote_copy(
            src_ref=source(i, kv, peer),
            dst_ref=target(i, kv, owner),
            send_sem=ctx_send.at[k],
            recv_sem=ctx_recv.at[k],
            device_id={"ctx": peer},
            device_id_type=MESH_ID,
        )

    def input_copy(turn, peer, owner):
        return pltpu.make_async_remote_copy(
            src_ref=source_columns(peer),
            dst_ref=input_block(owner),
            send_sem=dp_send.at[turn - 1],
            recv_sem=dp_recv.at[turn - 1],
            device_id={"dp": peer},
            device_id_type=MESH_ID,
        )

    def own(i, kv):
        return pltpu.make_async_copy(
            source(i, kv, ctx), target(i, kv, ctx), local_sems.at[kv * count + i]
        )

    own_input = pltpu.make_async_copy(
        source_columns(dp), input_block(dp), local_sems.at[kv_local * count]
    )

    def enter():
        barrier = pltpu.get_barrier_semaphore()
        for axis, me, size in (("ctx", ctx, n_ctx), ("dp", dp, n_dp)):
            for turn in range(1, size):
                pl.semaphore_signal(
                    barrier,
                    inc=1,
                    device_id={axis: lax.rem(me + turn, size)},
                    device_id_type=MESH_ID,
                )
        pl.semaphore_wait(barrier, n_ctx + n_dp - 2)
        for kv in range(kv_local):
            for i in range(count):
                for turn in range(1, n_ctx):
                    copy = ctx_copy(i, kv, turn, lax.rem(ctx + turn, n_ctx), ctx)
                    copy.start()
                    remote.append(copy)
                own(i, kv).start()
        for turn in range(1, n_dp):
            copy = input_copy(turn, lax.rem(dp + turn, n_dp), dp)
            copy.start()
            remote.append(copy)
        own_input.start()

    made = []

    def produce(column):
        while len(made) * (group + 2) * HEAD_DIM < column:
            kv = len(made)
            for i in range(count):
                own(i, kv).wait()
                for turn in range(1, n_ctx):
                    origin = lax.rem(ctx + n_ctx - turn, n_ctx)
                    ctx_copy(i, kv, turn, origin, origin).wait_recv()
            block = min(256, rows * n_ctx)
            head_grads(group, block, kv, *targets, grouped, dk_acc, dv_acc)
            made.append(kv)

    def relay():
        own_input.wait()
        for turn in range(1, n_dp):
            origin = lax.rem(dp + n_dp - turn, n_dp)
            input_copy(turn, origin, origin).wait_recv()
        for turn in range(1, n_ctx):
            copy = token_copy(turn, lax.rem(ctx + turn, n_ctx), ctx)
            copy.start()
            remote.append(copy)

    gather_kernel(
        *shape, grouped, out_ref, *rest[10:], enter=enter, produce=produce, relay=relay
    )
    for turn in range(1, n_ctx):
        origin = lax.rem(ctx + n_ctx - turn, n_ctx)
        token_copy(turn, origin, origin).wait_recv()
    for copy in remote:
        copy.wait_send()


def front(arrays, layer_input, n_ctx, n_dp):
    rows = layer_input.shape[0]
    length = rows * n_ctx
    widths = tuple(array.shape[1] // n_ctx for array in arrays)
    input_width = layer_input.shape[1] // n_dp
    columns = widths[0] + 2 * widths[1]
    kv_local = widths[1] // HEAD_DIM
    shape, semaphores = gather_plan(length, columns, n_dp)
    dma = pltpu.SemaphoreType.DMA
    ctx_copies = len(arrays) * (n_ctx - 1) * kv_local
    anywhere = pl.BlockSpec(memory_space=pl.ANY)
    return pl.pallas_call(
        functools.partial(front_kernel, n_ctx, n_dp, widths, input_width, shape),
        in_specs=[anywhere] * (len(arrays) + 1),
        out_specs=[anywhere] * 2,
        out_shape=[
            jax.ShapeDtypeStruct((n_dp, length, columns), jnp.bfloat16),
            jax.ShapeDtypeStruct((n_dp, length, input_width), jnp.bfloat16),
        ],
        scratch_shapes=[pltpu.VMEM((length, width), jnp.bfloat16) for width in widths]
        + [
            pltpu.VMEM((length, columns), jnp.bfloat16),
            pltpu.VMEM((length, HEAD_DIM), jnp.float32),
            pltpu.VMEM((length, HEAD_DIM), jnp.float32),
            dma((ctx_copies,)),
            dma((ctx_copies,)),
            dma((n_dp - 1,)),
            dma((n_dp - 1,)),
            dma((n_ctx - 1,)),
            dma((n_ctx - 1,)),
            dma((len(arrays) * kv_local + 1,)),
        ]
        + semaphores,
        compiler_params=pltpu.CompilerParams(
            collective_id=3, has_side_effects=True, vmem_limit_bytes=50 * 1024 * 1024
        ),
        cost_estimate=pl.CostEstimate(
            flops=10 * length * length * widths[0],
            bytes_accessed=4 * n_dp * length * columns,
            transcendentals=length * length * widths[0] // HEAD_DIM,
        ),
        name="front",
    )(*arrays, layer_input)


def total_kernel(n_ctx, n_dp, x_ref, out_ref, held_dp, part, held_ctx, *sems):
    dp_send, dp_recv, ctx_send, ctx_recv = sems
    dp = lax.axis_index("dp")
    ctx = lax.axis_index("ctx")
    stages = (
        ("dp", dp, n_dp, x_ref, held_dp, dp_send, dp_recv),
        ("ctx", ctx, n_ctx, part, held_ctx, ctx_send, ctx_recv),
    )
    barrier = pltpu.get_barrier_semaphore()
    for axis, me, size, *_ in stages:
        for turn in range(1, size):
            pl.semaphore_signal(
                barrier, inc=1, device_id={axis: lax.rem(me + turn, size)}, device_id_type=MESH_ID
            )
    pl.semaphore_wait(barrier, n_ctx + n_dp - 2)
    for axis, me, size, block, held, send, recv in stages:
        copies = [
            pltpu.make_async_remote_copy(
                src_ref=block,
                dst_ref=held.at[turn - 1],
                send_sem=send.at[turn - 1],
                recv_sem=recv.at[turn - 1],
                device_id={axis: lax.rem(me + turn, size)},
                device_id_type=MESH_ID,
            )
            for turn in range(1, size)
        ]
        for copy in copies:
            copy.start()
        for copy in copies:
            copy.wait()
        total = block[...]
        for turn in range(1, size):
            total += held[turn - 1]
        if axis == "dp":
            part[...] = total
        else:
            out_ref[...] = total


def total_over_devices(first, second, n_ctx, n_dp):
    rows = jnp.arange(8)[:, None]
    block = jnp.where(rows == 0, first, jnp.where(rows == 1, second, 0.0))
    block = jnp.broadcast_to(block, (8, 128)).astype(jnp.float32)
    dma = pltpu.SemaphoreType.DMA
    total = pl.pallas_call(
        functools.partial(total_kernel, n_ctx, n_dp),
        in_specs=[pl.BlockSpec(memory_space=pltpu.VMEM)],
        out_specs=pl.BlockSpec(memory_space=pltpu.VMEM),
        out_shape=jax.ShapeDtypeStruct((8, 128), jnp.float32),
        scratch_shapes=[
            pltpu.VMEM((n_dp - 1, 8, 128), jnp.float32),
            pltpu.VMEM((8, 128), jnp.float32),
            pltpu.VMEM((n_ctx - 1, 8, 128), jnp.float32),
            dma((n_dp - 1,)),
            dma((n_dp - 1,)),
            dma((n_ctx - 1,)),
            dma((n_ctx - 1,)),
        ],
        compiler_params=pltpu.CompilerParams(collective_id=4, has_side_effects=True),
        cost_estimate=pl.CostEstimate(flops=0, bytes_accessed=65536, transcendentals=0),
        name="total",
    )(block)
    return total[0, 0], total[1, 0]


def body(
    devices,
    heads_split,
    layer_input,
    queries,
    keys_saved,
    values_saved,
    out_grad,
    master_weight,
    first_moment,
    second_moment,
):
    weight_sq = jnp.sum(master_weight * master_weight)
    grouped_all, input_rows = front(
        (queries[0], keys_saved[0], values_saved[0], out_grad[0]),
        layer_input[0],
        heads_split,
        devices,
    )
    gradient = lax.dot_general(
        input_rows,
        grouped_all,
        (((0, 1), (0, 1)), ((), ())),
        preferred_element_type=jnp.float32,
    )
    first_new = beta_first * first_moment + (1.0 - beta_first) * gradient
    second_new = beta_second * second_moment + (1.0 - beta_second) * gradient * gradient
    corr_first = 1.0 - beta_first**STEP
    corr_second = 1.0 - beta_second**STEP
    direction = (
        first_new / corr_first / (jnp.sqrt(second_new / corr_second) + adam_epsilon)
        + decay_rate * master_weight
    )
    update_sq = jnp.sum(direction * direction)
    weight_total, update_total = total_over_devices(
        weight_sq, update_sq, heads_split, devices
    )
    trust_ratio = jnp.sqrt(weight_total) / jnp.sqrt(update_total)
    lamb_update = trust_ratio * direction
    new_local = (master_weight - learn_rate * lamb_update).astype(jnp.bfloat16)
    new_weights = gather_dp(new_local, devices, 2, "gather_weights")
    return (first_new, second_new, lamb_update, new_weights.reshape(-1, new_local.shape[1]))


def solution(mesh):
    in_specs = (
        P("dp", "ctx", None),
        P("dp", "ctx", None),
        P("dp", "ctx", None),
        P("dp", "ctx", None),
        P("dp", "ctx", None),
        P("dp", "ctx"),
        P("dp", "ctx"),
        P("dp", "ctx"),
    )
    out_specs = (P("dp", "ctx"), P("dp", "ctx"), P("dp", "ctx"), P(None, "ctx"))
    return jax.shard_map(
        functools.partial(body, mesh.shape["dp"], mesh.shape["ctx"]),
        mesh=mesh,
        in_specs=in_specs,
        out_specs=out_specs,
        check_vma=False,
    )
```
